256 devices in a mesh: wide: 32 (over y, z), narrow: 8 (over x, core).
Axes of the slice: x: 4, y: 4, z: 8, core: 2. Of those that a mesh axis runs over, the one named last changes fastest.
Arguments:
- point_feats: bfloat16 [64, 524288], P(None, ('wide', 'narrow')), may hold values from -6 to 6
- edge_offset: float32 [3, 8388608], P(None, ('wide', 'narrow')), may hold values from -1.5 to 1.5
- edge_point: int32 [65536, 128], P(('wide', 'narrow')), may hold values from 0 to 2047
- block_fill: int32 [65536], P(('wide', 'narrow')), may hold values from 1 to 128, as said below
- block_owner: int32 [65536, 1], P(('wide', 'narrow')), may hold values from 0 to 31; in each aligned block of 256 rows (0 to 255, 256 to 511, ...) at most 16 rows name the same one
- block_cell: int32 [65536], P(('wide', 'narrow')), may hold values from 0 to 8191
- enc_in_w: bfloat16 [128, 6], replicated, may hold values from -2.5 to 2.5
- enc_in_b: float32 [128], replicated, may hold values from -3 to 3
- enc_mid_w: bfloat16 [128, 128], replicated, may hold values from -0.5 to 0.5
- enc_mid_b: float32 [128], replicated, may hold values from -3 to 3
- enc_out_w: bfloat16 [64, 128], replicated, may hold values from -0.5 to 0.5
- point_proj: bfloat16 [64, 64], replicated, may hold values from -0.75 to 0.75
- dec_in_w: bfloat16 [128, 6], replicated, may hold values from -2.5 to 2.5
- dec_in_b: float32 [128], replicated, may hold values from -3 to 3
- dec_mid_w: bfloat16 [128, 128], replicated, may hold values from -0.5 to 0.5
- dec_mid_b: float32 [128], replicated, may hold values from -3 to 3
- dec_out_w: bfloat16 [64, 128], replicated, may hold values from -0.5 to 0.5
- cell_proj: bfloat16 [64, 64], replicated, may hold values from -0.75 to 0.75
- skip_weight: float32 [64, 64], replicated, may hold values from -0.75 to 0.75
- skip_bias: float32 [64], replicated, may hold values from -3 to 3
- spectral_weight: float32 [32, 32, 32, 64, 128], P('wide', None, 'narrow'), may hold values from -0.5 to 0.5
Outputs:
- decoded: bfloat16 [64, 524288], P(None, ('wide', 'narrow'))
The draws below stay inside these ranges and needn't reach their ends.
Inputs may be any that keep to these rules, and one draw needn't show every extreme that they name: `edge_point`: rows of a block name points of the device that holds the block. Rows r >= block_fill of a block are padding; every device holds a block with all 128 rows live. `block_owner`: the owner's narrow index is that of the device holding the block; among the 256 blocks of one device no wide index appears more than 16 times. `block_cell`: cell index within the owner's pencil of 4 x 128 / 8 x 128 cells, row-major.
All inputs are finite; a program needn't handle non-finite values.
Results may differ from the reference program's by a relative error of at most 0.0051.
Values may be sent and summed in bfloat16 or wider, within the bound.
A program may use at most 128 MiB of HBM per device.

```python
import math
import jax
import jax.numpy as jnp
import numpy as np
from jax import lax

C = 64
H = 128
G = 128
M = 32
ROWS = 128
PTS_DEV = 2048
BLK_DEV = 256
CAP = 16
POINTS = 524288
BLOCKS = 65536
EDGES = 8388608
CELLS_DEV = 8192
N_WIDE = 32
N_NARROW = 8


def draw_block_fill(key, part):
    key = jax.random.fold_in(key, 7)
    first_key, second_key, third_key = jax.random.split(key, 3)
    holders = BLOCKS // BLK_DEV
    partial_rows = jax.random.randint(first_key, (holders, BLK_DEV), 1, ROWS + 1)
    full_pick = jax.random.randint(second_key, (holders, BLK_DEV), 0, 10) < 3
    filled = jnp.where(full_pick, ROWS, partial_rows)
    chosen = jax.random.randint(third_key, (holders, 1), 0, BLK_DEV)
    filled = jnp.where(jnp.arange(BLK_DEV)[None, :] == chosen, ROWS, filled)
    return filled.reshape(BLOCKS).astype(jnp.int32)


def plant(result, rng, low, top_value):
    longest = result.shape.index(max(result.shape))
    spots = []
    for shift in (0, 1):
        where = [jax.random.randint(jax.random.fold_in(rng, axis), (), 0, length) for axis, length in enumerate(result.shape)]
        where[longest] = (where[longest] + shift) % result.shape[longest]
        spots.append(tuple(where))
    return result.at[spots[0]].set(low).at[spots[1]].set(top_value)


def level_of(own_key, dims, cuts, smallest, high):
    gain, own = 1.0, jax.random.fold_in(own_key, 6)
    for dim, parts in cuts:
        draws = jnp.exp(jax.random.uniform(jax.random.fold_in(own, dim), (parts,), jnp.float32, smallest / len(cuts), high / len(cuts)))
        gain = gain * jnp.repeat(draws, dims[dim] // parts).reshape([-1 if axis == dim else 1 for axis in range(len(dims))])
    return gain


def routed_block(stream_key, own, number, rows, count, top, reach, skew):
    ranking = jax.random.permutation(stream_key, count)
    crowded, usual = shares(count, rows * top, reach, skew, True), shares(count, rows * top, reach, skew, False)
    places = jnp.arange(count)

    def named(tallies, rotation):
        used = int((tallies > 0).sum())
        fixed = max(1, used // 4)
        shifted = fixed + (places - fixed + rotation * (used - fixed)) % max(1, count - fixed)
        return jnp.zeros((count,), jnp.int32).at[ranking[jnp.where(places < fixed, places, shifted)]].set(jnp.asarray(tallies, jnp.int32))

    tallies = jnp.where(number % 4 == 0, named(crowded, number // 4), named(usual, number - number // 4 - 1))
    mixed = jax.random.permutation(jax.random.fold_in(own, 3), count)
    donor, sink = mixed[0:count // 2 * 2:2], mixed[1:count // 2 * 2:2]
    slack = jnp.minimum(tallies[donor] - 1, reach - tallies[sink]) // 2
    slack = jnp.where((donor == ranking[0]) | (sink == ranking[0]) | (tallies[sink] == 0), 0, jnp.maximum(slack, 0))
    shifted = jax.random.randint(jax.random.fold_in(own, 4), (count // 2,), 0, 1 << 20) % (slack + 1)
    tallies = tallies.at[donor].add(-shifted).at[sink].add(shifted)
    items = jnp.searchsorted(jnp.cumsum(tallies), jnp.arange(rows * top), side="right").astype(jnp.int32)
    table = items.reshape(top, rows).T
    table = table[jax.random.permutation(jax.random.fold_in(own, 1), rows)]
    rotation = jax.random.randint(jax.random.fold_in(own, 2), (rows, 1), 0, top)
    return jnp.take_along_axis(table, (jnp.arange(top)[None, :] + rotation) % top, axis=1)


def shares(count, total, most, skew, full):
    weights = [(1 << 20) // math.isqrt(grade ** skew) + 1 for grade in range(1, count + 1)]
    largest = most if full else min(most, max(-(-total // count), total * weights[0] // sum(weights)))
    least = 1 if total - largest >= count - 1 else 0
    given, rest = [largest] + [least] * (count - 1), total - largest - least * (count - 1)
    while rest > 0:
        candidates = [i for i in range(1, count) if given[i] < largest] or [i for i in range(1, count) if given[i] < most]
        pool, left = sum([weights[i] for i in candidates]), rest
        for i in candidates:
            addition = min(most - given[i], max(1, left * weights[i] // pool), rest)
            given[i] = given[i] + addition
            rest = rest - addition
    return np.array(given)


def normal_values(key, shape, scale, bound, cuts=(), kind=jnp.bfloat16):
    drawn = scale * jax.random.normal(key, shape, jnp.float32)
    if cuts:
        drawn = drawn * level_of(key, shape, cuts, -0.22, 0.18)
    return jnp.clip(drawn, -bound, bound).astype(kind)


def setup_inputs(seed: int = 0) -> dict:
    arg_keys = jax.random.split(jax.random.key(seed), 22)
    point_feats = normal_values(arg_keys[0], (C, POINTS), 1.0, 6.0, ((1, 256),))
    edge_offset = jnp.clip(jax.random.uniform(arg_keys[1], (3, EDGES), jnp.float32, -1.5, 1.5) * level_of(arg_keys[1], (3, EDGES), ((1, 256),), -0.4, 0.0), -1.5, 1.5)
    edge_point = plant(jax.random.randint(arg_keys[2], (BLOCKS, ROWS), 0, PTS_DEV), jax.random.fold_in(arg_keys[2], 1), 0, PTS_DEV - 1).astype(jnp.int32)
    block_fill = draw_block_fill(jax.random.fold_in(arg_keys[21], 71), 0)
    block_owner_keys = jax.random.split(jax.random.fold_in(arg_keys[4], 1), BLOCKS // BLK_DEV)
    block_owner_turns = jax.random.permutation(jax.random.fold_in(arg_keys[4], 3), BLOCKS // BLK_DEV)
    block_owner = jax.vmap(lambda own, number: routed_block(jax.random.fold_in(arg_keys[4], 2), own, number, BLK_DEV, N_WIDE, 1, CAP, 2))(block_owner_keys, block_owner_turns).reshape((BLOCKS, 1))
    block_cell = plant(jax.random.randint(arg_keys[5], (BLOCKS,), 0, CELLS_DEV), jax.random.fold_in(arg_keys[5], 1), 0, CELLS_DEV - 1).astype(jnp.int32)
    enc_in_w = normal_values(arg_keys[6], (H, 6), 6 ** -0.5, 2.5)
    enc_in_b = normal_values(arg_keys[7], (H,), 0.5, 3.0, (), jnp.float32)
    enc_mid_w = normal_values(arg_keys[8], (H, H), H ** -0.5, 0.5)
    enc_mid_b = normal_values(arg_keys[9], (H,), 0.5, 3.0, (), jnp.float32)
    enc_out_w = normal_values(arg_keys[10], (C, H), H ** -0.5, 0.5)
    point_proj = normal_values(arg_keys[11], (C, C), C ** -0.5, 0.75)
    dec_in_w = normal_values(arg_keys[12], (H, 6), 6 ** -0.5, 2.5)
    dec_in_b = normal_values(arg_keys[13], (H,), 0.5, 3.0, (), jnp.float32)
    dec_mid_w = normal_values(arg_keys[14], (H, H), H ** -0.5, 0.5)
    dec_mid_b = normal_values(arg_keys[15], (H,), 0.5, 3.0, (), jnp.float32)
    dec_out_w = normal_values(arg_keys[16], (C, H), H ** -0.5, 0.5)
    cell_proj = normal_values(arg_keys[17], (C, C), C ** -0.5, 0.75)
    skip_weight = normal_values(arg_keys[18], (C, C), C ** -0.5, 0.75, (), jnp.float32)
    skip_bias = normal_values(arg_keys[19], (C,), 0.5, 3.0, (), jnp.float32)
    spectral_weight = normal_values(arg_keys[20], (M, M, M, C, 2 * C), (2 * C) ** -0.5, 0.5, ((0, 32), (2, 8)), jnp.float32)
    return {"point_feats": point_feats, "edge_offset": edge_offset, "edge_point": edge_point, "block_fill": block_fill, "block_owner": block_owner, "block_cell": block_cell, "enc_in_w": enc_in_w, "enc_in_b": enc_in_b, "enc_mid_w": enc_mid_w, "enc_mid_b": enc_mid_b, "enc_out_w": enc_out_w, "point_proj": point_proj, "dec_in_w": dec_in_w, "dec_in_b": dec_in_b, "dec_mid_w": dec_mid_w, "dec_mid_b": dec_mid_b, "dec_out_w": dec_out_w, "cell_proj": cell_proj, "skip_weight": skip_weight, "skip_bias": skip_bias, "spectral_weight": spectral_weight}


highest = lax.Precision.HIGHEST

def tables(length, number):
    position = jnp.arange(length, dtype=jnp.int32)
    waves = jnp.arange(number, dtype=jnp.int32) - number // 2
    phases = position[:, None] * waves[None, :] % length
    angles = phases.astype(jnp.float32) * (2.0 * math.pi / length)
    return (jnp.cos(angles), jnp.sin(angles))

def kernel(first_w, first_b, second_w, second_b, third_w, features):
    hidden = jax.nn.gelu(jnp.dot(first_w, features, preferred_element_type=jnp.float32) + first_b[:, None]).astype(jnp.bfloat16)
    hidden = jax.nn.gelu(jnp.dot(second_w, hidden, preferred_element_type=jnp.float32) + second_b[:, None]).astype(jnp.bfloat16)
    return jnp.dot(third_w, hidden, preferred_element_type=jnp.float32)

def einsum_high(form, left, right):
    return jnp.einsum(form, left, right, precision=highest)

def reference(point_feats, edge_offset, edge_point, block_fill, block_owner, block_cell, enc_in_w, enc_in_b, enc_mid_w, enc_mid_b, enc_out_w, point_proj, dec_in_w, dec_in_b, dec_mid_w, dec_mid_b, dec_out_w, cell_proj, skip_weight, skip_bias, spectral_weight):
    devices = N_WIDE * N_NARROW
    chans = point_feats.shape[0]
    x_local = G // N_WIDE
    y_local = G // N_NARROW
    edge_rows = BLK_DEV * ROWS
    feats = point_feats.reshape(chans, devices, PTS_DEV).transpose(1, 0, 2)
    offsets = edge_offset.reshape(3, devices, edge_rows).transpose(1, 0, 2)
    points = edge_point.reshape(devices, edge_rows)
    fills = block_fill.reshape(devices, BLK_DEV)
    owners = block_owner.reshape(devices, BLK_DEV)
    cell_ids = block_cell.reshape(devices, BLK_DEV)
    narrow_index = jnp.arange(devices, dtype=jnp.int32) % N_NARROW
    coord_x = owners * x_local + cell_ids // (y_local * G)
    coord_y = narrow_index[:, None] * y_local + cell_ids // G % y_local
    coord_z = cell_ids % G
    global_cell = ((coord_x * G + coord_y) * G + coord_z).astype(jnp.int32)
    centres = (2.0 * jnp.stack([coord_x, coord_y, coord_z], axis=1).astype(jnp.float32) + 1.0) / G - 1.0
    live_rows = (jnp.arange(ROWS, dtype=jnp.int32)[None, None, :] < fills[:, :, None]).reshape(devices, edge_rows)

    def edge_inputs(offset_rows, centre_rows):
        return jnp.concatenate([offset_rows, jnp.repeat(centre_rows, ROWS, axis=1)], axis=0).astype(jnp.bfloat16)

    def encode(operands):
        feat_rows, offset_rows, point_rows, centre_rows, live = operands
        weight = kernel(enc_in_w, enc_in_b, enc_mid_w, enc_mid_b, enc_out_w, edge_inputs(offset_rows, centre_rows))
        projected = jnp.dot(point_proj, feat_rows, preferred_element_type=jnp.float32).astype(jnp.bfloat16)
        picked = jnp.take(projected, point_rows, axis=1).astype(jnp.float32)
        message = jnp.where(live[None, :], weight * picked, jnp.zeros((), jnp.float32))
        return message.reshape(chans, BLK_DEV, ROWS).sum(axis=2)
    block_sums = lax.map(encode, (feats, offsets, points, centres, live_rows))
    flat_cells = global_cell.reshape(-1)
    totals = jax.ops.segment_sum(block_sums.transpose(0, 2, 1).reshape(-1, chans), flat_cells, num_segments=G * G * G)
    counts = jax.ops.segment_sum(fills.reshape(-1).astype(jnp.float32), flat_cells, num_segments=G * G * G)
    latent = (totals / jnp.maximum(jnp.sqrt(counts), 1.0)[:, None]).reshape(G, G, G, chans)
    cos_t, sin_t = tables(G, M)
    real_z = einsum_high('xyzc,zk->xykc', latent, cos_t)
    imag_z = -einsum_high('xyzc,zk->xykc', latent, sin_t)
    real_y = einsum_high('xykc,yj->xjkc', real_z, cos_t) + einsum_high('xykc,yj->xjkc', imag_z, sin_t)
    imag_y = einsum_high('xykc,yj->xjkc', imag_z, cos_t) - einsum_high('xykc,yj->xjkc', real_z, sin_t)
    real_x = einsum_high('xjkc,xi->jikc', real_y, cos_t) + einsum_high('xjkc,xi->jikc', imag_y, sin_t)
    imag_x = einsum_high('xjkc,xi->jikc', imag_y, cos_t) - einsum_high('xjkc,xi->jikc', real_y, sin_t)
    weight_real = spectral_weight[..., :chans]
    weight_imag = spectral_weight[..., chans:]
    out_real = einsum_high('jikc,jikcd->jikd', real_x, weight_real) - einsum_high('jikc,jikcd->jikd', imag_x, weight_imag)
    out_imag = einsum_high('jikc,jikcd->jikd', real_x, weight_imag) + einsum_high('jikc,jikcd->jikd', imag_x, weight_real)
    back_real = einsum_high('jikc,xi->xjkc', out_real, cos_t) - einsum_high('jikc,xi->xjkc', out_imag, sin_t)
    back_imag = einsum_high('jikc,xi->xjkc', out_imag, cos_t) + einsum_high('jikc,xi->xjkc', out_real, sin_t)
    grid_real = einsum_high('xjkc,yj->xykc', back_real, cos_t) - einsum_high('xjkc,yj->xykc', back_imag, sin_t)
    grid_imag = einsum_high('xjkc,yj->xykc', back_imag, cos_t) + einsum_high('xjkc,yj->xykc', back_real, sin_t)
    spectral = (einsum_high('xykc,zk->xyzc', grid_real, cos_t) - einsum_high('xykc,zk->xyzc', grid_imag, sin_t)) / (M * M * M)
    linear = einsum_high('xyzc,cd->xyzd', latent, skip_weight) + skip_bias
    field = jax.nn.gelu(spectral + linear).astype(jnp.bfloat16).reshape(G * G * G, chans)

    def decode(operands):
        offset_rows, point_rows, centre_rows, live, cell_rows = operands
        weight = kernel(dec_in_w, dec_in_b, dec_mid_w, dec_mid_b, dec_out_w, edge_inputs(offset_rows, centre_rows))
        values = jnp.take(field, cell_rows, axis=0)
        gathered = jnp.dot(cell_proj, values.T, preferred_element_type=jnp.float32)
        message = jnp.where(live[None, :], weight * jnp.repeat(gathered, ROWS, axis=1), jnp.zeros((), jnp.float32))
        point_sums = jax.ops.segment_sum(message.T, point_rows, num_segments=PTS_DEV)
        degree = jax.ops.segment_sum(live.astype(jnp.float32), point_rows, num_segments=PTS_DEV)
        return (point_sums / jnp.maximum(jnp.sqrt(degree), 1.0)[:, None]).T.astype(jnp.bfloat16)
    decoded = lax.map(decode, (offsets, points, centres, live_rows, global_cell))
    return decoded.transpose(1, 0, 2).reshape(chans, devices * PTS_DEV)
```

```python
import functools
import math

import jax
import jax.numpy as jnp
import numpy as np
from jax import lax
from jax.experimental import pallas as pl
from jax.experimental.pallas import tpu as pltpu
from jax.sharding import PartitionSpec as P

G = 128
M = 32
C = 64
H = 128
ROWS = 128
WIDE = 32
NARROW = 8
SLOTS = 16
ENTRIES = WIDE * SLOTS
XL = G // WIDE
YL = G // NARROW
KZ = M // NARROW
PTS = 2048
BLKS = 256
LOW = 256
HIGH = PTS // LOW
STEP_BLKS = 16
LANES = STEP_BLKS * ROWS
SUB = 256
BF = jnp.bfloat16
F32 = jnp.float32

NT = (((1,), (1,)), ((), ()))
TN = (((0,), (0,)), ((), ()))


def dot(left, right, dims=(((1,), (0,)), ((), ()))):
    return lax.dot_general(left, right, dims, preferred_element_type=F32)


def angles(positions, waves):
    return 2.0 * np.pi * (np.outer(positions, waves) % G) / G


WAVES = np.arange(M) - M // 2


def z_table():
    turn = angles(np.arange(G), WAVES)
    both = np.stack([np.cos(turn), -np.sin(turn)], axis=2)
    return np.repeat(both.reshape(G, 2 * M), C, axis=1).astype(BF)


def y_forward_table():
    turn = angles(WAVES, np.arange(G))
    return np.concatenate([np.cos(turn), np.sin(turn)], axis=0).astype(BF)


def y_inverse_table():
    turn = angles(np.arange(G), WAVES)
    return np.concatenate([np.cos(turn), np.sin(turn)], axis=0).astype(BF)


def x_forward_table():
    turn = angles(WAVES, np.arange(G))
    same = np.eye(KZ)
    halves = []
    for wave in (np.cos(turn), np.sin(turn)):
        full = np.einsum("ix,kl->ikxl", wave, same)
        full = np.repeat(full[:, None], 2, axis=1)
        halves.append(full.reshape(M * 2 * KZ, G * KZ))
    return np.concatenate(halves, axis=0).astype(BF)


def x_inverse_table():
    turn = angles(np.arange(G), WAVES)
    same = np.eye(KZ)
    cos, sin = np.cos(turn) / M**3, np.sin(turn) / M**3
    halves = []
    for first, second in ((cos, -sin), (sin, cos)):
        full = np.einsum("xis,kl->xkisl", np.stack([first, second], axis=2), same)
        halves.append(full.reshape(G * KZ, M * 2 * KZ))
    return np.concatenate(halves, axis=0).astype(BF)


def half_gelu(half):
    slope = math.sqrt(2.0 / math.pi)
    inner = half * (half * half * (8.0 * slope * 0.044715) + 2.0 * slope)
    return half + half * jnp.tanh(inner)


def turned(value):
    lane = lax.broadcasted_iota(jnp.int32, value.shape, 1)
    rolled = pltpu.roll(value, C, 1)
    return jnp.where(lane < C, -rolled, rolled)


def network(first_w, second_w, second_b, third_w, features):
    hidden = half_gelu(dot(first_w, features)).astype(BF)
    bias = jnp.concatenate([second_b] * (features.shape[1] // second_b.shape[1]), axis=1)
    hidden = half_gelu(dot(second_w, hidden) + bias).astype(BF)
    return dot(third_w, hidden)


def block_lanes():
    lane = lax.broadcasted_iota(jnp.int32, (STEP_BLKS, LANES), 1)
    return lane - lax.broadcasted_iota(jnp.int32, (STEP_BLKS, LANES), 0) * ROWS


def edge_features(offsets_ref, centres_ref, distance, features_ref):
    inside = jnp.where((distance >= 0) & (distance < ROWS), 1.0, 0.0).astype(BF)
    features_ref[...] = dot(centres_ref[0], inside)
    features_ref[0:3, :] = offsets_ref[...]
    return features_ref[...].astype(BF)


def point_rows(points_ref, sub):
    per = SUB // ROWS
    return jnp.concatenate([points_ref[sub * per + i : sub * per + i + 1, :] for i in range(per)], axis=1)


def low_onehot(row, iota_ref):
    low = jnp.broadcast_to((row & (LOW - 1)).astype(F32), (16, SUB)).astype(BF)
    low = jnp.concatenate([low] * (LOW // 16), axis=0)
    return jnp.where(low == iota_ref[...], jnp.ones((), BF), jnp.zeros((), BF))


def fill_iota(iota_ref):
    iota_ref[...] = lax.broadcasted_iota(jnp.int32, (LOW, SUB), 0).astype(F32).astype(BF)


def encode_body(
    owner_row, owner_col, meta, feats, proj, w1, w2, b2, w3, centres, fill, offsets, points,
    sent, grouped, sums, features, iota,
):
    step = pl.program_id(0)

    @pl.when(step == 0)
    def _():
        projected = dot(proj[...], feats[...]).astype(BF)
        for high in range(HIGH):
            grouped[high * C : (high + 1) * C, :] = projected[:, high * LOW : (high + 1) * LOW]
        fill_iota(iota)
        sums[...] = meta[...]

    distance = block_lanes()
    live = jnp.where((distance >= 0) & (distance < fill[...]), 1.0, 0.0).astype(BF)
    inputs = edge_features(offsets, centres, distance, features)
    messages = []
    for sub in range(LANES // SUB):
        lanes = slice(sub * SUB, (sub + 1) * SUB)
        weight = network(w1[...], w2[...], b2[...], w3[...], inputs[:, lanes])
        row = point_rows(points, sub)
        spread = dot(grouped[...], low_onehot(row, iota))
        high_row = jnp.broadcast_to(row >> 8, (C, SUB))
        picked = spread[0:C]
        for high in range(1, HIGH):
            picked = jnp.where(high_row == high, spread[high * C : (high + 1) * C], picked)
        messages.append((weight * picked).astype(BF))
    message = jnp.concatenate(messages, axis=1)
    rows = pl.ds(pl.multiple_of(step * STEP_BLKS, STEP_BLKS), STEP_BLKS)
    sums[rows, 0:C] = dot(live, message, NT)

    @pl.when(step == BLKS // STEP_BLKS - 1)
    def _():
        before = lax.broadcasted_iota(jnp.int32, (BLKS, BLKS), 0) < lax.broadcasted_iota(
            jnp.int32, (BLKS, BLKS), 1
        )
        same = owner_col[...] == owner_row[...]
        rank = jnp.sum(jnp.where(same & before, 1, 0), axis=0, keepdims=True)
        target = owner_row[...] * SLOTS + rank
        slot = lax.broadcasted_iota(jnp.int32, (ENTRIES, BLKS), 0)
        placer = jnp.where(slot == target, 1.0, 0.0).astype(BF)
        sent[...] = dot(placer, sums[...].astype(BF)).astype(BF)


def entry_cells(received):
    cell_row = received[:, C : C + 1].astype(F32)
    cell_z = received[:, C + 1 : C + 2].astype(F32)
    lane = lax.broadcasted_iota(jnp.int32, (16, 2 * C), 1)
    sub = lax.broadcasted_iota(jnp.int32, (16, 2 * C), 0)
    picker = jnp.where(lane == sub + C, 1.0, 0.0).astype(BF)
    rows = dot(picker, received, NT)
    return cell_row, cell_z, rows[0:1, :], rows[1:2, :]


def forward_z_body(received_ref, table, out, latent):
    received = received_ref[...]
    cell_row, cell_z, row_xy, row_z = entry_cells(received)
    same = (cell_row * G + cell_z) == (row_xy * G + row_z)
    totals = dot(jnp.where(same, 1.0, 0.0).astype(BF), received)
    scale = 1.0 / jnp.maximum(jnp.sqrt(totals[:, C + 2 : C + 3]), 1.0)
    latent[...] = totals * scale
    own = received.astype(F32) * scale
    lane = lax.broadcasted_iota(jnp.int32, own.shape, 1)
    own = jnp.where(lane < C, own, pltpu.roll(own, C, 1))
    position = lax.broadcasted_iota(jnp.int32, (ENTRIES, G), 1).astype(F32)
    at_z = jnp.where(position == cell_z, 1.0, 0.0).astype(BF)
    pencil = lax.broadcasted_iota(jnp.int32, (XL * YL, ENTRIES), 0).astype(F32)
    at_row = jnp.where(pencil == row_xy, 1.0, 0.0).astype(BF)
    width = KZ * 2 * C
    spread = jnp.concatenate([own] * KZ, axis=1)
    for group in range(NARROW):
        phases = dot(at_z, table[:, group * width : (group + 1) * width])
        modes = dot(at_row, (spread * phases).astype(BF)).astype(BF)
        for x in range(XL):
            out[group, :, x * width : (x + 1) * width] = modes[x * YL : (x + 1) * YL, :]


def forward_y_body(received, table, out, columns):
    both = dot(table[...], received[...])
    for j in range(XL * KZ):
        lanes = slice(j * 2 * C, (j + 1) * 2 * C)
        columns[pl.ds(j, M, stride=XL * KZ), :] = both[0:M, lanes] - turned(both[M:, lanes])
    out[...] = columns[...].astype(BF)


def x_body(received, forward, inverse, weight, out, left, product):
    count = M * 2 * KZ
    both = dot(forward[...], received[...])
    modes = both[0:count] - turned(both[count:])
    row = lax.broadcasted_iota(jnp.int32, (count, 2 * C), 0)
    lane = lax.broadcasted_iota(jnp.int32, (count, 2 * C), 1)
    real_row = (row // KZ) % 2 == 0
    wide = jnp.where(real_row == (lane < C), modes, pltpu.roll(modes, C, 1))
    for half in range(KZ // 2):
        keep = row % KZ == 2 * half + lane // C
        left[:, half * 2 * C : (half + 1) * 2 * C] = jnp.where(keep, wide, 0.0)
    for kx in range(M):
        rows = slice(kx * 2 * KZ, (kx + 1) * 2 * KZ)
        mixer = weight[kx].reshape(KZ * C, 2 * C).astype(BF)
        product[rows, :] = dot(left[rows, :].astype(BF), mixer)
    back = dot(inverse[...], product[...].astype(BF))
    cells = G * KZ
    out[...] = (back[0:cells] + turned(back[cells:])).astype(BF)


def inverse_y_body(received, table, out, columns):
    columns[...] = received[...].astype(F32)
    for j in range(XL * KZ):
        column = columns[pl.ds(j, M, stride=XL * KZ), :].astype(BF)
        both = dot(table[...], column)
        value = both[0:G] + turned(both[G:])
        out[:, j * 2 * C : (j + 1) * 2 * C] = value.astype(BF)


def inverse_z_body(received_ref, latent, spectra, table, skip, bias, out):
    received = received_ref[...]
    cell_row = received[:, C : C + 1].astype(F32)
    cell_z = received[:, C + 1 : C + 2].astype(F32)
    position = lax.broadcasted_iota(jnp.int32, (ENTRIES, G), 1).astype(F32)
    at_z = jnp.where(position == cell_z, 1.0, 0.0).astype(BF)
    pencil = lax.broadcasted_iota(jnp.int32, (ENTRIES, XL * YL), 1).astype(F32)
    at_row = jnp.where(pencil == cell_row, 1.0, 0.0).astype(BF)
    width = KZ * 2 * C
    total = jnp.zeros((ENTRIES, 2 * C), F32)
    for group in range(NARROW):
        phases = dot(at_z, table[:, group * width : (group + 1) * width])
        pencils = jnp.concatenate(
            [spectra[group, :, x * width : (x + 1) * width] for x in range(XL)], axis=0
        )
        terms = phases * dot(at_row, pencils)
        for j in range(KZ):
            total += terms[:, j * 2 * C : (j + 1) * 2 * C]
    spectral = total[:, 0:C] + total[:, C:]
    linear = jnp.dot(latent[:, 0:C], skip[...], precision=lax.Precision.HIGHEST, preferred_element_type=F32)
    field = half_gelu(0.5 * (spectral + linear + bias[...]))
    out[...] = jnp.concatenate([field, jnp.zeros_like(field)], axis=1).astype(BF)


def decode_body(
    owner_row, owner_col, returned, proj, w1, w2, b2, w3, centres, fill, offsets, points,
    out, gathered, totals, features, iota,
):
    step = pl.program_id(0)

    @pl.when(step == 0)
    def _():
        before = lax.broadcasted_iota(jnp.int32, (BLKS, BLKS), 1) < lax.broadcasted_iota(
            jnp.int32, (BLKS, BLKS), 0
        )
        same = owner_col[...] == owner_row[...]
        rank = jnp.sum(jnp.where(same & before, 1, 0), axis=1, keepdims=True)
        target = owner_col[...] * SLOTS + rank
        slot = lax.broadcasted_iota(jnp.int32, (BLKS, ENTRIES), 1)
        picker = jnp.where(slot == target, 1.0, 0.0).astype(BF)
        values = dot(picker, returned[...]).astype(BF)
        gathered[...] = dot(values[:, 0:C], proj[...], NT)
        fill_iota(iota)
        totals[...] = jnp.zeros_like(totals)

    distance = block_lanes()
    live = jnp.where((distance >= 0) & (distance < fill[...]), 1.0, 0.0)
    alive = jnp.sum(live, axis=0, keepdims=True)
    live = live.astype(BF)
    inputs = edge_features(offsets, centres, distance, features)
    rows = pl.ds(pl.multiple_of(step * STEP_BLKS, STEP_BLKS), STEP_BLKS)
    cells = gathered[rows, :]
    cells_high = cells.astype(BF)
    cells_low = (cells - cells_high.astype(F32)).astype(BF)
    pieces = jnp.concatenate([cells_high, cells_low], axis=0)
    live = jnp.concatenate([live, live], axis=0)
    for sub in range(LANES // SUB):
        lanes = slice(sub * SUB, (sub + 1) * SUB)
        weight = network(w1[...], w2[...], b2[...], w3[...], inputs[:, lanes])
        message = (weight * dot(pieces, live[:, lanes], TN)).astype(BF)
        row = point_rows(points, sub)
        high = jnp.broadcast_to((row >> 8).astype(F32), (16, SUB)).astype(BF)
        high_rows = jnp.concatenate([high] * (C // 16), axis=0)
        parts = [
            jnp.where(high_rows == jnp.full((), i, BF), message, jnp.zeros((), BF)) for i in range(HIGH)
        ]
        number = lax.broadcasted_iota(jnp.int32, (16, SUB), 0)
        count = jnp.where(number == row >> 8, jnp.broadcast_to(alive[:, lanes], (16, SUB)), 0.0)
        parts.append(count.astype(BF))
        totals[...] += dot(jnp.concatenate(parts, axis=0), low_onehot(row, iota), NT)

    @pl.when(step == BLKS // STEP_BLKS - 1)
    def _():
        for high in range(HIGH):
            degree = totals[HIGH * C + high : HIGH * C + high + 1, :]
            scale = 1.0 / jnp.maximum(jnp.sqrt(degree), 1.0)
            value = totals[high * C : (high + 1) * C, :] * scale
            out[:, high * LOW : (high + 1) * LOW] = value.astype(BF)


def whole(shape):
    return pl.BlockSpec(shape, lambda i: (0,) * len(shape))


def edge_specs():
    return [
        whole((H, 16)),
        whole((H, H)),
        whole((H, ROWS)),
        whole((C, H)),
        pl.BlockSpec((1, 16, STEP_BLKS), lambda i: (i, 0, 0)),
        pl.BlockSpec((STEP_BLKS, 1), lambda i: (i, 0)),
        pl.BlockSpec((3, LANES), lambda i: (0, i)),
        pl.BlockSpec((STEP_BLKS, ROWS), lambda i: (i, 0)),
    ]


PARAMS = pltpu.CompilerParams(vmem_limit_bytes=40 * 1024 * 1024)


def call(body, shapes, scratch=()):
    return pl.pallas_call(
        body,
        out_shape=[jax.ShapeDtypeStruct(shape, kind) for shape, kind in shapes],
        scratch_shapes=list(scratch),
        compiler_params=PARAMS,
        name=body.__name__,
    )


def network_weights(in_w, in_b, mid_w, mid_b, out_w):
    half_b = 0.5 * in_b
    high = half_b.astype(BF)
    low = (half_b - high.astype(F32)).astype(BF)
    first = jnp.concatenate(
        [0.5 * in_w, high[:, None], low[:, None], jnp.zeros((H, 8), BF)], axis=1
    ).astype(BF)
    second_b = jnp.broadcast_to(0.5 * mid_b[:, None], (H, ROWS))
    return first, (0.5 * mid_w).astype(BF), second_b, out_w


def shards(
    point_feats,
    edge_offset,
    edge_point,
    block_fill,
    block_owner,
    block_cell,
    enc_in_w,
    enc_in_b,
    enc_mid_w,
    enc_mid_b,
    enc_out_w,
    point_proj,
    dec_in_w,
    dec_in_b,
    dec_mid_w,
    dec_mid_b,
    dec_out_w,
    cell_proj,
    skip_weight,
    skip_bias,
    spectral_weight,
):
    narrow_here = lax.axis_index("narrow")
    owners = block_owner[:, 0]
    coord_x = owners * XL + block_cell // (YL * G)
    coord_y = narrow_here * YL + block_cell // G % YL
    coord_z = block_cell % G
    coords = jnp.stack([coord_x, coord_y, coord_z], axis=0).astype(F32)
    centres = ((2.0 * coords + 1.0) / G - 1.0).astype(BF)
    steps = BLKS // STEP_BLKS
    tall = jnp.concatenate(
        [jnp.zeros((3, BLKS), BF), centres, jnp.ones((2, BLKS), BF), jnp.zeros((8, BLKS), BF)], axis=0
    )
    tall = tall.reshape(16, steps, STEP_BLKS).transpose(1, 0, 2)
    owner_row = owners[None, :]
    fill_col = block_fill[:, None]
    facts = jnp.stack([block_cell // G, coord_z, block_fill], axis=1).astype(F32)
    meta = jnp.pad(facts, ((0, 0), (C, C - 3)))

    scratch = [pltpu.VMEM((16, LANES), F32), pltpu.VMEM((LOW, SUB), BF)]
    arbitrary = pltpu.CompilerParams(
        vmem_limit_bytes=40 * 1024 * 1024, dimension_semantics=("arbitrary",)
    )
    sent = pl.pallas_call(
        encode_body,
        grid=(steps,),
        out_shape=jax.ShapeDtypeStruct((ENTRIES, 2 * C), BF),
        in_specs=[
            whole((1, BLKS)),
            whole((BLKS, 1)),
            whole((BLKS, 2 * C)),
            whole((C, PTS)),
            whole((C, C)),
        ]
        + edge_specs(),
        out_specs=whole((ENTRIES, 2 * C)),
        scratch_shapes=[pltpu.VMEM((HIGH * C, LOW), BF), pltpu.VMEM((BLKS, 2 * C), F32)] + scratch,
        compiler_params=arbitrary,
        name="encode",
    )(
        owner_row,
        block_owner,
        meta,
        point_feats,
        point_proj,
        *network_weights(enc_in_w, enc_in_b, enc_mid_w, enc_mid_b, enc_out_w),
        tall,
        fill_col,
        edge_offset,
        edge_point,
    )

    def swap(value, axis, count):
        value = value.reshape(count, value.size // count // value.shape[-1], value.shape[-1])
        return lax.all_to_all(value, axis, split_axis=0, concat_axis=0, tiled=True)

    table_z = jnp.asarray(z_table())
    received = swap(sent, "wide", WIDE).reshape(ENTRIES, 2 * C)
    pencils, latent = call(
        forward_z_body, [((NARROW, YL, XL * KZ * 2 * C), BF), ((ENTRIES, 2 * C), F32)]
    )(received, table_z)
    columns = swap(pencils, "narrow", NARROW).reshape(G, XL * KZ * 2 * C)
    work = pltpu.VMEM((M * XL * KZ, 2 * C), F32)
    (y_modes,) = call(forward_y_body, [((M * XL * KZ, 2 * C), BF)], [work])(
        columns, jnp.asarray(y_forward_table())
    )
    slabs = swap(y_modes, "wide", WIDE).reshape(G * KZ, 2 * C)
    (mixed,) = call(
        x_body,
        [((G * KZ, 2 * C), BF)],
        [pltpu.VMEM((M * 2 * KZ, KZ * C), F32), pltpu.VMEM((M * 2 * KZ, 2 * C), F32)],
    )(slabs, jnp.asarray(x_forward_table()), jnp.asarray(x_inverse_table()), spectral_weight[0])
    rows = swap(mixed, "wide", WIDE).reshape(M * XL * KZ, 2 * C)
    (grid_modes,) = call(inverse_y_body, [((G, XL * KZ * 2 * C), BF)], [work])(
        rows, jnp.asarray(y_inverse_table())
    )
    spectra = swap(grid_modes, "narrow", NARROW)
    (reply,) = call(inverse_z_body, [((ENTRIES, 2 * C), BF)])(
        received, latent, spectra, table_z, skip_weight, skip_bias[None, :]
    )
    returned = swap(reply, "wide", WIDE).reshape(ENTRIES, 2 * C)
    return pl.pallas_call(
        decode_body,
        grid=(steps,),
        out_shape=jax.ShapeDtypeStruct((C, PTS), BF),
        in_specs=[whole((1, BLKS)), whole((BLKS, 1)), whole((ENTRIES, 2 * C)), whole((C, C))]
        + edge_specs(),
        out_specs=whole((C, PTS)),
        scratch_shapes=[pltpu.VMEM((BLKS, C), F32), pltpu.VMEM((HIGH * C + 16, LOW), F32)] + scratch,
        compiler_params=arbitrary,
        name="decode",
    )(
        owner_row,
        block_owner,
        returned,
        cell_proj,
        *network_weights(dec_in_w, dec_in_b, dec_mid_w, dec_mid_b, dec_out_w),
        tall,
        fill_col,
        edge_offset,
        edge_point,
    )


def solution(mesh):
    return jax.shard_map(
        shards,
        mesh=mesh,
        in_specs=(
            P(None, ("wide", "narrow")),
            P(None, ("wide", "narrow")),
            P(("wide", "narrow"), None),
            P(("wide", "narrow")),
            P(("wide", "narrow"), None),
            P(("wide", "narrow")),
            P(),
            P(),
            P(),
            P(),
            P(),
            P(),
            P(),
            P(),
            P(),
            P(),
            P(),
            P(),
            P(),
            P(),
            P("wide", None, "narrow", None, None),
        ),
        out_specs=P(None, ("wide", "narrow")),
        check_vma=False,
    )
```

```python
import functools
import math

import jax
import jax.numpy as jnp
import numpy as np
from jax import lax
from jax.experimental import pallas as pl
from jax.experimental.pallas import tpu as pltpu
from jax.sharding import PartitionSpec as P

G = 128
M = 32
C = 64
H = 128
ROWS = 128
WIDE = 32
NARROW = 8
SLOTS = 16
ENTRIES = WIDE * SLOTS
XL = G // WIDE
YL = G // NARROW
KZ = M // NARROW
PTS = 2048
BLKS = 256
LOW = 256
HIGH = PTS // LOW
STEP_BLKS = 16
LANES = STEP_BLKS * ROWS
BF = jnp.bfloat16
F32 = jnp.float32

NT = (((1,), (1,)), ((), ()))
TN = (((0,), (0,)), ((), ()))


def dot(left, right, dims=(((1,), (0,)), ((), ()))):
    return lax.dot_general(left, right, dims, preferred_element_type=F32)


def angles(positions, waves):
    return 2.0 * np.pi * (np.outer(positions, waves) % G) / G


WAVES = np.arange(M) - M // 2


def z_table():
    turn = angles(np.arange(G), WAVES)
    both = np.stack([np.cos(turn), -np.sin(turn)], axis=2)
    return np.repeat(both.reshape(G, 2 * M), C, axis=1).astype(BF)


def y_forward_table():
    turn = angles(WAVES, np.arange(G))
    return np.concatenate([np.cos(turn), np.sin(turn)], axis=0).astype(BF)


def y_inverse_table():
    turn = angles(np.arange(G), WAVES)
    return np.concatenate([np.cos(turn), np.sin(turn)], axis=0).astype(BF)


def x_forward_table():
    turn = angles(WAVES, np.arange(G))
    same = np.eye(KZ)
    halves = []
    for wave in (np.cos(turn), np.sin(turn)):
        full = np.einsum("ix,kl->ikxl", wave, same)
        full = np.repeat(full[:, None], 2, axis=1)
        halves.append(full.reshape(M * 2 * KZ, G * KZ))
    return np.concatenate(halves, axis=0).astype(BF)


def x_inverse_table():
    turn = angles(np.arange(G), WAVES)
    same = np.eye(KZ)
    cos, sin = np.cos(turn) / M**3, np.sin(turn) / M**3
    halves = []
    for first, second in ((cos, -sin), (sin, cos)):
        full = np.einsum("xis,kl->xkisl", np.stack([first, second], axis=2), same)
        halves.append(full.reshape(G * KZ, M * 2 * KZ))
    return np.concatenate(halves, axis=0).astype(BF)


def half_gelu(half):
    slope = math.sqrt(2.0 / math.pi)
    inner = half * (half * half * (8.0 * slope * 0.044715) + 2.0 * slope)
    return half + half * jnp.tanh(inner)


def turned(value):
    lane = lax.broadcasted_iota(jnp.int32, value.shape, 1)
    rolled = pltpu.roll(value, C, 1)
    return jnp.where(lane < C, -rolled, rolled)


def column_of(row):
    count = row.shape[1]
    down = lax.broadcasted_iota(jnp.int32, (count, count), 0)
    across = lax.broadcasted_iota(jnp.int32, (count, count), 1)
    return jnp.sum(jnp.where(down == across, row, jnp.zeros_like(row)), axis=1, keepdims=True)


def prepare_network(in_w, in_b, mid_w, mid_b, first, second, second_b):
    bias = 0.5 * column_of(in_b[...])
    high = bias.astype(BF).astype(F32)
    lane = lax.broadcasted_iota(jnp.int32, (H, 16), 1)
    first[...] = jnp.where(lane == 6, high, jnp.where(lane == 7, bias - high, 0.0))
    first[:, 0:6] = 0.5 * in_w[...].astype(F32)
    second[...] = (0.5 * mid_w[...].astype(F32)).astype(BF)
    second_b[...] = jnp.broadcast_to(0.5 * column_of(mid_b[...]), (H, ROWS))


def network(first, second, second_b, third_w, features):
    hidden = half_gelu(dot(first[...].astype(BF), features)).astype(BF)
    bias = jnp.concatenate([second_b[...]] * (features.shape[1] // ROWS), axis=1)
    hidden = half_gelu(dot(second[...], hidden) + bias).astype(BF)
    return dot(third_w[...], hidden)


FILL, OWNER, META = 8, 9, C


def prepare_blocks(owner, cell, fill, blocks):
    cell_row, cell_z = cell[...] >> 7, cell[...] & (G - 1)
    coord_x = owner[...] * XL + (cell_row >> 4)
    coord_y = lax.axis_index("narrow") * YL + (cell_row & (YL - 1))
    number = lax.broadcasted_iota(jnp.int32, (2 * C, BLKS), 0)
    facts = jnp.where((number == 6) | (number == 7), 1.0, 0.0)
    rows = [(3 + i, (2.0 * at.astype(F32) + 1.0) / G - 1.0) for i, at in enumerate((coord_x, coord_y, cell_z))]
    rows += [(FILL, fill[...]), (OWNER, owner[...]), (META, cell_row), (META + 1, cell_z), (META + 2, fill[...])]
    for place, value in rows:
        facts = jnp.where(number == place, value.astype(F32), facts)
    blocks[...] = facts.T


def block_lanes():
    lane = lax.broadcasted_iota(jnp.int32, (STEP_BLKS, LANES), 1)
    return lane - lax.broadcasted_iota(jnp.int32, (STEP_BLKS, LANES), 0) * ROWS


def edge_features(offsets_ref, facts, distance, features_ref):
    inside = jnp.where((distance >= 0) & (distance < ROWS), 1.0, 0.0).astype(BF)
    features_ref[...] = dot(facts[:, 0:16].astype(BF), inside, TN)
    features_ref[0:3, :] = offsets_ref[...]
    return features_ref[...].astype(BF)


def live_lanes(facts, distance):
    fill = facts[:, FILL : FILL + 1].astype(jnp.int32)
    return jnp.where((distance >= 0) & (distance < fill), 1.0, 0.0)


def point_row(points_ref):
    return jnp.concatenate([points_ref[i : i + 1, :] for i in range(STEP_BLKS)], axis=1)


def low_onehot(row):
    low = jnp.broadcast_to((row & (LOW - 1)).astype(F32), (16, LANES)).astype(BF)
    low = jnp.concatenate([low] * (LOW // 16), axis=0)
    number = lax.broadcasted_iota(jnp.int32, (LOW, LANES), 0).astype(F32).astype(BF)
    return jnp.where(low == number, jnp.ones((), BF), jnp.zeros((), BF))


def encode_body(
    owner, cell, fill, feats, proj, in_w, in_b, mid_w, mid_b, out_w, offsets, points,
    sent, grouped, sums, blocks, features, first, second, second_b,
):
    step = pl.program_id(0)

    @pl.when(step == 0)
    def _():
        projected = dot(proj[...], feats[...]).astype(BF)
        for high in range(HIGH):
            grouped[high * C : (high + 1) * C, :] = projected[:, high * LOW : (high + 1) * LOW]
        prepare_blocks(owner, cell, fill, blocks)
        prepare_network(in_w, in_b, mid_w, mid_b, first, second, second_b)
        sums[...] = blocks[...]

    rows = pl.ds(pl.multiple_of(step * STEP_BLKS, STEP_BLKS), STEP_BLKS)
    facts = blocks[rows, :]
    distance = block_lanes()
    live = live_lanes(facts, distance).astype(BF)
    weight = network(first, second, second_b, out_w, edge_features(offsets, facts, distance, features))
    row = point_row(points)
    spread = dot(grouped[...], low_onehot(row))
    high_row = jnp.broadcast_to(row >> 8, (C, LANES))
    picked = spread[0:C]
    for high in range(1, HIGH):
        picked = jnp.where(high_row == high, spread[high * C : (high + 1) * C], picked)
    sums[rows, 0:C] = dot(live, (weight * picked).astype(BF), NT)

    @pl.when(step == BLKS // STEP_BLKS - 1)
    def _():
        before = lax.broadcasted_iota(jnp.int32, (BLKS, BLKS), 0) < lax.broadcasted_iota(
            jnp.int32, (BLKS, BLKS), 1
        )
        same = blocks[:, OWNER : OWNER + 1].astype(jnp.int32) == owner[...]
        rank = jnp.sum(jnp.where(same & before, 1, 0), axis=0, keepdims=True)
        target = owner[...] * SLOTS + rank
        slot = lax.broadcasted_iota(jnp.int32, (ENTRIES, BLKS), 0)
        placer = jnp.where(slot == target, 1.0, 0.0).astype(BF)
        sent[...] = dot(placer, sums[...].astype(BF)).astype(BF).reshape(sent.shape)


def entry_cells(received):
    cell_row = received[:, C : C + 1].astype(F32)
    cell_z = received[:, C + 1 : C + 2].astype(F32)
    lane = lax.broadcasted_iota(jnp.int32, (16, 2 * C), 1)
    sub = lax.broadcasted_iota(jnp.int32, (16, 2 * C), 0)
    picker = jnp.where(lane == sub + C, 1.0, 0.0).astype(BF)
    rows = dot(picker, received, NT)
    return cell_row, cell_z, rows[0:1, :], rows[1:2, :]


def exchange(axis, count, source, target, send_sem, recv_sem):
    me = lax.axis_index(axis)

    def copy(ahead, peer):
        return pltpu.make_async_remote_copy(
            src_ref=source.at[peer],
            dst_ref=target.at[me],
            send_sem=send_sem.at[ahead],
            recv_sem=recv_sem.at[ahead],
            device_id={axis: peer},
            device_id_type=pl.DeviceIdType.MESH,
        )

    def each(action):
        def step(ahead, carry):
            action(copy(ahead, lax.rem(me + ahead, count)))
            return carry

        lax.fori_loop(1, count, step, 0)

    def start():
        each(lambda one: one.start())
        target[me] = source[me]

    return start, lambda: each(lambda one: one.wait_recv()), lambda: each(lambda one: one.wait_send())


def greet():
    barrier = pltpu.get_barrier_semaphore()
    for axis, count in (("wide", WIDE), ("narrow", NARROW)):
        me = lax.axis_index(axis)

        def step(ahead, carry):
            pl.semaphore_signal(
                barrier,
                inc=1,
                device_id={axis: lax.rem(me + ahead, count)},
                device_id_type=pl.DeviceIdType.MESH,
            )
            return carry

        lax.fori_loop(1, count, step, 0)
    pl.semaphore_wait(barrier, WIDE + NARROW - 2)


def forward_z(received_ref, table, out, latent):
    received = received_ref[...].reshape(ENTRIES, 2 * C)
    cell_row, cell_z, row_xy, row_z = entry_cells(received)
    same = (cell_row * G + cell_z) == (row_xy * G + row_z)
    totals = dot(jnp.where(same, 1.0, 0.0).astype(BF), received)
    scale = 1.0 / jnp.maximum(jnp.sqrt(totals[:, C + 2 : C + 3]), 1.0)
    latent[...] = totals * scale
    own = received.astype(F32) * scale
    lane = lax.broadcasted_iota(jnp.int32, own.shape, 1)
    own = jnp.where(lane < C, own, pltpu.roll(own, C, 1))
    position = lax.broadcasted_iota(jnp.int32, (ENTRIES, G), 1).astype(F32)
    at_z = jnp.where(position == cell_z, 1.0, 0.0).astype(BF)
    pencil = lax.broadcasted_iota(jnp.int32, (XL * YL, ENTRIES), 0).astype(F32)
    at_row = jnp.where(pencil == row_xy, 1.0, 0.0).astype(BF)
    width = KZ * 2 * C
    spread = jnp.concatenate([own] * KZ, axis=1)
    for group in range(NARROW):
        phases = dot(at_z, table[:, group * width : (group + 1) * width])
        modes = dot(at_row, (spread * phases).astype(BF)).astype(BF)
        for x in range(XL):
            out[group, :, x * width : (x + 1) * width] = modes[x * YL : (x + 1) * YL, :]


def forward_y(received, table, out, columns):
    both = dot(table[...], received[...].reshape(G, XL * KZ * 2 * C))
    for j in range(XL * KZ):
        lanes = slice(j * 2 * C, (j + 1) * 2 * C)
        columns[pl.ds(j, M, stride=XL * KZ), :] = both[0:M, lanes] - turned(both[M:, lanes])
    out[...] = columns[...].astype(BF).reshape(out.shape)


def mix_x(received, forward, inverse, weight, out, left, product):
    count = M * 2 * KZ
    both = dot(forward[...], received[...].reshape(G * KZ, 2 * C))
    modes = both[0:count] - turned(both[count:])
    row = lax.broadcasted_iota(jnp.int32, (count, 2 * C), 0)
    lane = lax.broadcasted_iota(jnp.int32, (count, 2 * C), 1)
    real_row = (row // KZ) % 2 == 0
    wide = jnp.where(real_row == (lane < C), modes, pltpu.roll(modes, C, 1))
    for half in range(KZ // 2):
        keep = row % KZ == 2 * half + lane // C
        left[:, half * 2 * C : (half + 1) * 2 * C] = jnp.where(keep, wide, 0.0)
    for kx in range(M):
        rows = slice(kx * 2 * KZ, (kx + 1) * 2 * KZ)
        mixer = weight[kx].reshape(KZ * C, 2 * C).astype(BF)
        product[rows, :] = dot(left[rows, :].astype(BF), mixer)
    back = dot(inverse[...], product[...].astype(BF))
    cells = G * KZ
    out[...] = (back[0:cells] + turned(back[cells:])).astype(BF).reshape(out.shape)


def inverse_y(received, table, out, columns):
    columns[...] = received[...].reshape(M * XL * KZ, 2 * C).astype(F32)
    for j in range(XL * KZ):
        column = columns[pl.ds(j, M, stride=XL * KZ), :].astype(BF)
        both = dot(table[...], column)
        value = both[0:G] + turned(both[G:])
        out[:, :, j * 2 * C : (j + 1) * 2 * C] = value.astype(BF).reshape(NARROW, YL, 2 * C)


def inverse_z(received_ref, latent, spectra, table, skip, bias, out):
    received = received_ref[...].reshape(ENTRIES, 2 * C)
    cell_row = received[:, C : C + 1].astype(F32)
    cell_z = received[:, C + 1 : C + 2].astype(F32)
    position = lax.broadcasted_iota(jnp.int32, (ENTRIES, G), 1).astype(F32)
    at_z = jnp.where(position == cell_z, 1.0, 0.0).astype(BF)
    pencil = lax.broadcasted_iota(jnp.int32, (ENTRIES, XL * YL), 1).astype(F32)
    at_row = jnp.where(pencil == cell_row, 1.0, 0.0).astype(BF)
    width = KZ * 2 * C
    total = jnp.zeros((ENTRIES, 2 * C), F32)
    for group in range(NARROW):
        phases = dot(at_z, table[:, group * width : (group + 1) * width])
        pencils = jnp.concatenate(
            [spectra[group, :, x * width : (x + 1) * width] for x in range(XL)], axis=0
        )
        terms = phases * dot(at_row, pencils)
        for j in range(KZ):
            total += terms[:, j * 2 * C : (j + 1) * 2 * C]
    spectral = total[:, 0:C] + total[:, C:]
    linear = jnp.dot(latent[:, 0:C], skip[...], precision=lax.Precision.HIGHEST, preferred_element_type=F32)
    field = half_gelu(0.5 * (spectral + linear + bias[...]))
    field = jnp.concatenate([field, jnp.zeros_like(field)], axis=1)
    out[...] = field.astype(BF).reshape(out.shape)


WIDE_BUFFER = (WIDE, SLOTS, 2 * C)
NARROW_BUFFER = (NARROW, YL, XL * KZ * 2 * C)


def middle_body(
    sent, table_z, forward_y_t, forward_x_t, inverse_x_t, inverse_y_t, weight_hbm, skip, bias,
    returned, entries, pencils, columns, y_modes, slabs, mixed, rows, grid, spectra, reply,
    work, latent, left, product, weight, weight_sem, wide_send, wide_recv, narrow_send, narrow_recv,
):
    fetch = pltpu.make_async_copy(weight_hbm, weight, weight_sem)
    fetch.start()
    greet()

    def wide(number, source, target):
        return exchange("wide", WIDE, source, target, wide_send.at[number], wide_recv.at[number])

    def narrow(number, source, target):
        return exchange("narrow", NARROW, source, target, narrow_send.at[number], narrow_recv.at[number])

    sends = []

    def move(start, receive, sent_all):
        start()
        sends.append(sent_all)
        receive()

    move(*wide(0, sent, entries))
    forward_z(entries, table_z, pencils, latent)
    move(*narrow(0, pencils, columns))
    forward_y(columns, forward_y_t, y_modes, work)
    move(*wide(1, y_modes, slabs))
    fetch.wait()
    mix_x(slabs, forward_x_t, inverse_x_t, weight, mixed, left, product)
    move(*wide(2, mixed, rows))
    inverse_y(rows, inverse_y_t, grid, work)
    move(*narrow(1, grid, spectra))
    inverse_z(entries, latent, spectra, table_z, skip, bias, reply)
    move(*wide(3, reply, returned))
    for sent_all in sends:
        sent_all()


def decode_body(
    owner, cell, fill, returned, proj, in_w, in_b, mid_w, mid_b, out_w, offsets, points,
    out, gathered, totals, blocks, features, first, second, second_b,
):
    step = pl.program_id(0)

    @pl.when(step == 0)
    def _():
        prepare_blocks(owner, cell, fill, blocks)
        prepare_network(in_w, in_b, mid_w, mid_b, first, second, second_b)
        before = lax.broadcasted_iota(jnp.int32, (BLKS, BLKS), 1) < lax.broadcasted_iota(
            jnp.int32, (BLKS, BLKS), 0
        )
        own = blocks[:, OWNER : OWNER + 1].astype(jnp.int32)
        rank = jnp.sum(jnp.where((own == owner[...]) & before, 1, 0), axis=1, keepdims=True)
        target = own * SLOTS + rank
        slot = lax.broadcasted_iota(jnp.int32, (BLKS, ENTRIES), 1)
        picker = jnp.where(slot == target, 1.0, 0.0).astype(BF)
        values = dot(picker, returned[...].reshape(ENTRIES, 2 * C)).astype(BF)
        gathered[...] = dot(values[:, 0:C], proj[...], NT)
        totals[...] = jnp.zeros_like(totals)

    rows = pl.ds(pl.multiple_of(step * STEP_BLKS, STEP_BLKS), STEP_BLKS)
    facts = blocks[rows, :]
    distance = block_lanes()
    live = live_lanes(facts, distance)
    alive = jnp.sum(live, axis=0, keepdims=True)
    live = live.astype(BF)
    cells = gathered[rows, :]
    cells_high = cells.astype(BF)
    cells_low = (cells - cells_high.astype(F32)).astype(BF)
    pieces = jnp.concatenate([cells_high, cells_low], axis=0)
    weight = network(first, second, second_b, out_w, edge_features(offsets, facts, distance, features))
    message = (weight * dot(pieces, jnp.concatenate([live, live], axis=0), TN)).astype(BF)
    row = point_row(points)
    high = jnp.broadcast_to((row >> 8).astype(F32), (16, LANES)).astype(BF)
    high_rows = jnp.concatenate([high] * (C // 16), axis=0)
    parts = [jnp.where(high_rows == jnp.full((), i, BF), message, jnp.zeros((), BF)) for i in range(HIGH)]
    number = lax.broadcasted_iota(jnp.int32, (16, LANES), 0)
    count = jnp.where(number == row >> 8, jnp.broadcast_to(alive, (16, LANES)), 0.0)
    parts.append(count.astype(BF))
    totals[...] += dot(jnp.concatenate(parts, axis=0), low_onehot(row), NT)

    @pl.when(step == BLKS // STEP_BLKS - 1)
    def _():
        for high in range(HIGH):
            degree = totals[HIGH * C + high : HIGH * C + high + 1, :]
            scale = 1.0 / jnp.maximum(jnp.sqrt(degree), 1.0)
            value = totals[high * C : (high + 1) * C, :] * scale
            out[:, high * LOW : (high + 1) * LOW] = value.astype(BF)


def whole(shape):
    return pl.BlockSpec(shape, lambda i: (0,) * len(shape))


def edge_specs():
    return [
        whole((H, 6)),
        whole((1, H)),
        whole((H, H)),
        whole((1, H)),
        whole((C, H)),
        pl.BlockSpec((3, LANES), lambda i: (0, i)),
        pl.BlockSpec((STEP_BLKS, ROWS), lambda i: (i, 0)),
    ]


STEPS = BLKS // STEP_BLKS
PARAMS = dict(vmem_limit_bytes=48 * 1024 * 1024)
EDGE_SCRATCH = [
    pltpu.VMEM((BLKS, 2 * C), F32),
    pltpu.VMEM((16, LANES), F32),
    pltpu.VMEM((H, 16), F32),
    pltpu.VMEM((H, H), BF),
    pltpu.VMEM((H, ROWS), F32),
]


def encode_call():
    return pl.pallas_call(
        encode_body,
        grid=(STEPS,),
        out_shape=jax.ShapeDtypeStruct(WIDE_BUFFER, BF),
        in_specs=[whole((1, BLKS))] * 3 + [whole((C, PTS)), whole((C, C))] + edge_specs(),
        out_specs=whole(WIDE_BUFFER),
        scratch_shapes=[pltpu.VMEM((HIGH * C, LOW), BF), pltpu.VMEM((BLKS, 2 * C), F32)] + EDGE_SCRATCH,
        compiler_params=pltpu.CompilerParams(dimension_semantics=("arbitrary",), **PARAMS),
        name="encode",
    )


def decode_call():
    return pl.pallas_call(
        decode_body,
        grid=(STEPS,),
        out_shape=jax.ShapeDtypeStruct((C, PTS), BF),
        in_specs=[whole((1, BLKS))] * 3 + [whole(WIDE_BUFFER), whole((C, C))] + edge_specs(),
        out_specs=whole((C, PTS)),
        scratch_shapes=[pltpu.VMEM((BLKS, C), F32), pltpu.VMEM((HIGH * C + 16, LOW), F32)] + EDGE_SCRATCH,
        compiler_params=pltpu.CompilerParams(dimension_semantics=("arbitrary",), **PARAMS),
        name="decode",
    )


def middle_call():
    vmem = pl.BlockSpec(memory_space=pltpu.VMEM)
    wide, narrow = pltpu.VMEM(WIDE_BUFFER, BF), pltpu.VMEM(NARROW_BUFFER, BF)
    return pl.pallas_call(
        middle_body,
        out_shape=jax.ShapeDtypeStruct(WIDE_BUFFER, BF),
        in_specs=[vmem] * 6 + [pl.BlockSpec(memory_space=pl.ANY)] + [vmem] * 2,
        out_specs=vmem,
        scratch_shapes=[
            wide, narrow, narrow, wide, wide, wide, wide, narrow, narrow, wide,
            pltpu.VMEM((M * XL * KZ, 2 * C), F32),
            pltpu.VMEM((ENTRIES, 2 * C), F32),
            pltpu.VMEM((M * 2 * KZ, KZ * C), F32),
            pltpu.VMEM((M * 2 * KZ, 2 * C), F32),
            pltpu.VMEM((M, KZ, C, 2 * C), F32),
            pltpu.SemaphoreType.DMA,
            pltpu.SemaphoreType.DMA((4, WIDE)),
            pltpu.SemaphoreType.DMA((4, WIDE)),
            pltpu.SemaphoreType.DMA((2, NARROW)),
            pltpu.SemaphoreType.DMA((2, NARROW)),
        ],
        compiler_params=pltpu.CompilerParams(collective_id=0, has_side_effects=True, **PARAMS),
        name="middle",
    )


def shards(
    point_feats,
    edge_offset,
    edge_point,
    block_fill,
    block_owner,
    block_cell,
    enc_in_w,
    enc_in_b,
    enc_mid_w,
    enc_mid_b,
    enc_out_w,
    point_proj,
    dec_in_w,
    dec_in_b,
    dec_mid_w,
    dec_mid_b,
    dec_out_w,
    cell_proj,
    skip_weight,
    skip_bias,
    spectral_weight,
):
    blocks = (block_owner.reshape(1, BLKS), block_cell[None, :], block_fill[None, :])
    edges = (edge_offset, edge_point)
    sent = encode_call()(
        *blocks, point_feats, point_proj,
        enc_in_w, enc_in_b[None, :], enc_mid_w, enc_mid_b[None, :], enc_out_w, *edges,
    )
    tables = (z_table(), y_forward_table(), x_forward_table(), x_inverse_table(), y_inverse_table())
    returned = middle_call()(
        sent, *[jnp.asarray(table) for table in tables], spectral_weight[0], skip_weight, skip_bias[None, :]
    )
    return decode_call()(
        *blocks, returned, cell_proj,
        dec_in_w, dec_in_b[None, :], dec_mid_w, dec_mid_b[None, :], dec_out_w, *edges,
    )


def solution(mesh):
    return jax.shard_map(
        shards,
        mesh=mesh,
        in_specs=(
            P(None, ("wide", "narrow")),
            P(None, ("wide", "narrow")),
            P(("wide", "narrow"), None),
            P(("wide", "narrow")),
            P(("wide", "narrow"), None),
            P(("wide", "narrow")),
            P(),
            P(),
            P(),
            P(),
            P(),
            P(),
            P(),
            P(),
            P(),
            P(),
            P(),
            P(),
            P(),
            P(),
            P("wide", None, "narrow", None, None),
        ),
        out_specs=P(None, ("wide", "narrow")),
        check_vma=False,
    )
```

```python
import functools
import math

import jax
import jax.numpy as jnp
import numpy as np
from jax import lax
from jax.experimental import pallas as pl
from jax.experimental.pallas import tpu as pltpu
from jax.sharding import PartitionSpec as P

G = 128
M = 32
C = 64
H = 128
ROWS = 128
WIDE = 32
NARROW = 8
SLOTS = 16
ENTRIES = WIDE * SLOTS
XL = G // WIDE
YL = G // NARROW
KZ = M // NARROW
PTS = 2048
BLKS = 256
LOW = 256
HIGH = PTS // LOW
STEP_BLKS = 32
LANES = STEP_BLKS * ROWS
STEPS = BLKS // STEP_BLKS
BF = jnp.bfloat16
F32 = jnp.float32

NT = (((1,), (1,)), ((), ()))
TN = (((0,), (0,)), ((), ()))


def dot(left, right, dims=(((1,), (0,)), ((), ()))):
    return lax.dot_general(left, right, dims, preferred_element_type=F32)


def angles(positions, waves):
    return 2.0 * np.pi * (np.outer(positions, waves) % G) / G


WAVES = np.arange(M) - M // 2


def z_table():
    turn = angles(np.arange(G), WAVES)
    both = np.stack([np.cos(turn), -np.sin(turn)], axis=2)
    return np.repeat(both.reshape(G, 2 * M), C, axis=1).astype(BF)


def y_forward_table():
    turn = angles(WAVES, np.arange(G))
    return np.concatenate([np.cos(turn), np.sin(turn)], axis=0).astype(BF)


def y_inverse_table():
    turn = angles(np.arange(G), WAVES)
    return np.concatenate([np.cos(turn), np.sin(turn)], axis=0).astype(BF)


def x_forward_table():
    turn = angles(WAVES, np.arange(G))
    same = np.eye(KZ)
    halves = []
    for wave in (np.cos(turn), np.sin(turn)):
        full = np.einsum("ix,kl->ikxl", wave, same)
        full = np.repeat(full[:, None], 2, axis=1)
        halves.append(full.reshape(M * 2 * KZ, G * KZ))
    return np.concatenate(halves, axis=0).astype(BF)


def x_inverse_table():
    turn = angles(np.arange(G), WAVES)
    same = np.eye(KZ)
    cos, sin = np.cos(turn) / M**3, np.sin(turn) / M**3
    halves = []
    for first, second in ((cos, -sin), (sin, cos)):
        full = np.einsum("xis,kl->xkisl", np.stack([first, second], axis=2), same)
        halves.append(full.reshape(G * KZ, M * 2 * KZ))
    return np.concatenate(halves, axis=0).astype(BF)


def half_gelu(half):
    slope = math.sqrt(2.0 / math.pi)
    inner = half * (half * half * (8.0 * slope * 0.044715) + 2.0 * slope)
    return half + half * jnp.tanh(inner)


def turned(value):
    lane = lax.broadcasted_iota(jnp.int32, value.shape, 1)
    rolled = pltpu.roll(value, C, 1)
    return jnp.where(lane < C, -rolled, rolled)


def prepare_network(in_w, in_b, mid_w, mid_b, turned_w, first, second, second_b):
    bias = 0.5 * in_b[...]
    high = bias.astype(BF).astype(F32)
    number = lax.broadcasted_iota(jnp.int32, (H, H), 0)
    turned_w[...] = jnp.where(number == 6, high, jnp.where(number == 7, bias - high, 0.0))
    turned_w[0:6, :] = 0.5 * in_w[...].astype(F32)
    first[...] = turned_w[...].T.astype(BF)
    second[...] = (0.5 * mid_w[...].astype(F32)).astype(BF)
    second_b[...] = jnp.broadcast_to(0.5 * mid_b[...], (H, H)).T


def network(first, second, second_b, third_w, features):
    hidden = half_gelu(dot(first[:, 0:16], features)).astype(BF)
    bias = jnp.concatenate([second_b[...]] * (features.shape[1] // ROWS), axis=1)
    hidden = half_gelu(dot(second[...], hidden) + bias).astype(BF)
    return dot(third_w[...], hidden)


FILL, OWNER, META = 8, 9, C


def prepare_blocks(owner, cell, fill, blocks):
    cell_row, cell_z = cell[...] >> 7, cell[...] & (G - 1)
    coord_x = owner[...] * XL + (cell_row >> 4)
    coord_y = lax.axis_index("narrow") * YL + (cell_row & (YL - 1))
    number = lax.broadcasted_iota(jnp.int32, (2 * C, BLKS), 0)
    facts = jnp.where((number == 6) | (number == 7), 1.0, 0.0)
    rows = [(3 + i, (2.0 * at.astype(F32) + 1.0) / G - 1.0) for i, at in enumerate((coord_x, coord_y, cell_z))]
    rows += [(FILL, fill[...]), (OWNER, owner[...]), (META, cell_row), (META + 1, cell_z), (META + 2, fill[...])]
    for place, value in rows:
        facts = jnp.where(number == place, value.astype(F32), facts)
    blocks[...] = facts.T


def block_lanes():
    lane = lax.broadcasted_iota(jnp.int32, (STEP_BLKS, LANES), 1)
    return lane - lax.broadcasted_iota(jnp.int32, (STEP_BLKS, LANES), 0) * ROWS


def edge_features(offsets, facts, distance, features_ref):
    inside = jnp.where((distance >= 0) & (distance < ROWS), 1.0, 0.0).astype(BF)
    features_ref[...] = dot(facts[:, 0:16].astype(BF), inside, TN)
    features_ref[0:3, :] = offsets
    return features_ref[...].astype(BF)


def live_lanes(facts, distance):
    fill = facts[:, FILL : FILL + 1].astype(jnp.int32)
    return jnp.where((distance >= 0) & (distance < fill), 1.0, 0.0)


def chunk(step):
    return pl.ds(pl.multiple_of(step * STEP_BLKS, STEP_BLKS), STEP_BLKS)


def point_row(points):
    return jnp.concatenate([points[i : i + 1, :] for i in range(STEP_BLKS)], axis=1)


def low_onehot(row):
    low = jnp.broadcast_to((row & (LOW - 1)).astype(F32), (16, LANES)).astype(BF)
    low = jnp.concatenate([low] * (LOW // 16), axis=0)
    number = lax.broadcasted_iota(jnp.int32, (LOW, LANES), 0).astype(F32).astype(BF)
    return jnp.where(low == number, jnp.ones((), BF), jnp.zeros((), BF))


def project_points(proj, feats, grouped):
    projected = dot(proj[...], feats[...]).astype(BF)
    for high in range(HIGH):
        grouped[high * C : (high + 1) * C, :] = projected[:, high * LOW : (high + 1) * LOW]


def chunk_inputs(step, offsets, blocks, features):
    facts = blocks[chunk(step), :]
    distance = block_lanes()
    lanes = pl.ds(pl.multiple_of(step * LANES, LANES), LANES)
    return edge_features(offsets[:, lanes], facts, distance, features), live_lanes(facts, distance)


def encode_chunk(step, offsets, points, blocks, features, grouped, layers, sums):
    row = point_row(points[chunk(step), :])
    spread = dot(grouped[...], low_onehot(row))
    inputs, live = chunk_inputs(step, offsets, blocks, features)
    weight = network(*layers, inputs)
    high_row = jnp.broadcast_to(row >> 8, (C, LANES))
    picked = spread[0:C]
    for high in range(1, HIGH):
        picked = jnp.where(high_row == high, spread[high * C : (high + 1) * C], picked)
    sums[chunk(step), 0:C] = dot(live.astype(BF), (weight * picked).astype(BF), NT)


def pack_sums(owner, blocks, sums, sent):
    before = lax.broadcasted_iota(jnp.int32, (BLKS, BLKS), 0) < lax.broadcasted_iota(
        jnp.int32, (BLKS, BLKS), 1
    )
    same = blocks[:, OWNER : OWNER + 1].astype(jnp.int32) == owner[...]
    rank = jnp.sum(jnp.where(same & before, 1, 0), axis=0, keepdims=True)
    target = owner[...] * SLOTS + rank
    slot = lax.broadcasted_iota(jnp.int32, (ENTRIES, BLKS), 0)
    placer = jnp.where(slot == target, 1.0, 0.0).astype(BF)
    sent[...] = dot(placer, sums[...].astype(BF)).astype(BF).reshape(sent.shape)


def unpack_values(owner, blocks, returned, proj, gathered):
    before = lax.broadcasted_iota(jnp.int32, (BLKS, BLKS), 1) < lax.broadcasted_iota(
        jnp.int32, (BLKS, BLKS), 0
    )
    own = blocks[:, OWNER : OWNER + 1].astype(jnp.int32)
    rank = jnp.sum(jnp.where((own == owner[...]) & before, 1, 0), axis=1, keepdims=True)
    target = own * SLOTS + rank
    slot = lax.broadcasted_iota(jnp.int32, (BLKS, ENTRIES), 1)
    picker = jnp.where(slot == target, 1.0, 0.0).astype(BF)
    values = dot(picker, returned[...].reshape(ENTRIES, 2 * C)).astype(BF)
    gathered[...] = dot(values[:, 0:C], proj[...], NT)


def decode_chunk(step, points, blocks, weights, gathered, totals):
    live = live_lanes(blocks[chunk(step), :], block_lanes())
    alive = jnp.sum(live, axis=0, keepdims=True)
    live = live.astype(BF)
    cells = gathered[chunk(step), :]
    cells_high = cells.astype(BF)
    cells_low = (cells - cells_high.astype(F32)).astype(BF)
    pieces = jnp.concatenate([cells_high, cells_low], axis=0)
    spread = dot(pieces, jnp.concatenate([live, live], axis=0), TN)
    message = (weights[step] * spread).astype(BF)
    row = point_row(points[chunk(step), :])
    high = jnp.broadcast_to((row >> 8).astype(F32), (16, LANES)).astype(BF)
    high_rows = jnp.concatenate([high] * (C // 16), axis=0)
    parts = [jnp.where(high_rows == jnp.full((), i, BF), message, jnp.zeros((), BF)) for i in range(HIGH)]
    number = lax.broadcasted_iota(jnp.int32, (16, LANES), 0)
    count = jnp.where(number == row >> 8, jnp.broadcast_to(alive, (16, LANES)), 0.0)
    parts.append(count.astype(BF))
    totals[...] += dot(jnp.concatenate(parts, axis=0), low_onehot(row), NT)


def finish_points(totals, out):
    for high in range(HIGH):
        degree = totals[HIGH * C + high : HIGH * C + high + 1, :]
        scale = 1.0 / jnp.maximum(jnp.sqrt(degree), 1.0)
        value = totals[high * C : (high + 1) * C, :] * scale
        out[:, high * LOW : (high + 1) * LOW] = value.astype(BF)


def entry_cells(received):
    cell_row = received[:, C : C + 1].astype(F32)
    cell_z = received[:, C + 1 : C + 2].astype(F32)
    lane = lax.broadcasted_iota(jnp.int32, (16, 2 * C), 1)
    sub = lax.broadcasted_iota(jnp.int32, (16, 2 * C), 0)
    picker = jnp.where(lane == sub + C, 1.0, 0.0).astype(BF)
    rows = dot(picker, received, NT)
    return cell_row, cell_z, rows[0:1, :], rows[1:2, :]


def exchange(axis, count, source, target, send_sem, recv_sem):
    me = lax.axis_index(axis)

    def copy(ahead, peer):
        return pltpu.make_async_remote_copy(
            src_ref=source.at[peer],
            dst_ref=target.at[me],
            send_sem=send_sem.at[ahead],
            recv_sem=recv_sem.at[ahead],
            device_id={axis: peer},
            device_id_type=pl.DeviceIdType.MESH,
        )

    def each(action):
        def step(ahead, carry):
            action(copy(ahead, lax.rem(me + ahead, count)))
            return carry

        lax.fori_loop(1, count, step, 0)

    def start():
        each(lambda one: one.start())
        target[me] = source[me]

    return start, lambda: each(lambda one: one.wait_recv()), lambda: each(lambda one: one.wait_send())


def greet():
    barrier = pltpu.get_barrier_semaphore()
    for axis, count in (("wide", WIDE), ("narrow", NARROW)):
        me = lax.axis_index(axis)

        def step(ahead, carry):
            pl.semaphore_signal(
                barrier,
                inc=1,
                device_id={axis: lax.rem(me + ahead, count)},
                device_id_type=pl.DeviceIdType.MESH,
            )
            return carry

        lax.fori_loop(1, count, step, 0)
    return lambda: pl.semaphore_wait(barrier, WIDE + NARROW - 2)


def entry_phases(received_ref, table, phases):
    cell_z = received_ref[...].reshape(ENTRIES, 2 * C)[:, C + 1 : C + 2].astype(F32)
    position = lax.broadcasted_iota(jnp.int32, (ENTRIES, G), 1).astype(F32)
    at_z = jnp.where(position == cell_z, 1.0, 0.0).astype(BF)
    phases[...] = dot(at_z, table[...]).astype(BF)


def forward_z(received_ref, table, out, latent):
    received = received_ref[...].reshape(ENTRIES, 2 * C)
    cell_row, cell_z, row_xy, row_z = entry_cells(received)
    same = (cell_row * G + cell_z) == (row_xy * G + row_z)
    totals = dot(jnp.where(same, 1.0, 0.0).astype(BF), received)
    scale = 1.0 / jnp.maximum(jnp.sqrt(totals[:, C + 2 : C + 3]), 1.0)
    latent[...] = totals * scale
    own = received.astype(F32) * scale
    lane = lax.broadcasted_iota(jnp.int32, own.shape, 1)
    own = jnp.where(lane < C, own, pltpu.roll(own, C, 1))
    position = lax.broadcasted_iota(jnp.int32, (ENTRIES, G), 1).astype(F32)
    at_z = jnp.where(position == cell_z, 1.0, 0.0).astype(BF)
    pencil = lax.broadcasted_iota(jnp.int32, (XL * YL, ENTRIES), 0).astype(F32)
    at_row = jnp.where(pencil == row_xy, 1.0, 0.0).astype(BF)
    width = KZ * 2 * C
    spread = jnp.concatenate([own] * KZ, axis=1)
    for group in range(NARROW):
        phases = dot(at_z, table[:, group * width : (group + 1) * width])
        modes = dot(at_row, (spread * phases).astype(BF)).astype(BF)
        for x in range(XL):
            out[group, :, x * width : (x + 1) * width] = modes[x * YL : (x + 1) * YL, :]


def forward_y(received, table, out, columns):
    both = dot(table[...], received[...].reshape(G, XL * KZ * 2 * C))
    for j in range(XL * KZ):
        lanes = slice(j * 2 * C, (j + 1) * 2 * C)
        columns[pl.ds(j, M, stride=XL * KZ), :] = both[0:M, lanes] - turned(both[M:, lanes])
    out[...] = columns[...].astype(BF).reshape(out.shape)


def mix_x(received, forward, inverse, weight, out, left, product):
    count = M * 2 * KZ
    both = dot(forward[...], received[...].reshape(G * KZ, 2 * C))
    modes = both[0:count] - turned(both[count:])
    row = lax.broadcasted_iota(jnp.int32, (count, 2 * C), 0)
    lane = lax.broadcasted_iota(jnp.int32, (count, 2 * C), 1)
    real_row = (row // KZ) % 2 == 0
    wide = jnp.where(real_row == (lane < C), modes, pltpu.roll(modes, C, 1))
    for half in range(KZ // 2):
        keep = row % KZ == 2 * half + lane // C
        left[:, half * 2 * C : (half + 1) * 2 * C] = jnp.where(keep, wide, 0.0)
    for kx in range(M):
        rows = slice(kx * 2 * KZ, (kx + 1) * 2 * KZ)
        product[rows, :] = dot(left[rows, :].astype(BF), weight[kx])
    back = dot(inverse[...], product[...].astype(BF))
    cells = G * KZ
    out[...] = (back[0:cells] + turned(back[cells:])).astype(BF).reshape(out.shape)


def inverse_y(received, table, out, columns):
    columns[...] = received[...].reshape(M * XL * KZ, 2 * C).astype(F32)
    for j in range(XL * KZ):
        column = columns[pl.ds(j, M, stride=XL * KZ), :].astype(BF)
        both = dot(table[...], column)
        value = both[0:G] + turned(both[G:])
        out[:, :, j * 2 * C : (j + 1) * 2 * C] = value.astype(BF).reshape(NARROW, YL, 2 * C)


def inverse_z(received_ref, linear, spectra, phases, out):
    cell_row = received_ref[...].reshape(ENTRIES, 2 * C)[:, C : C + 1].astype(F32)
    pencil = lax.broadcasted_iota(jnp.int32, (ENTRIES, XL * YL), 1).astype(F32)
    at_row = jnp.where(pencil == cell_row, 1.0, 0.0).astype(BF)
    width = KZ * 2 * C
    total = jnp.zeros((ENTRIES, 2 * C), F32)
    for group in range(NARROW):
        pencils = jnp.concatenate(
            [spectra[group, :, x * width : (x + 1) * width] for x in range(XL)], axis=0
        )
        terms = phases[:, group * width : (group + 1) * width].astype(F32) * dot(at_row, pencils)
        for j in range(KZ):
            total += terms[:, j * 2 * C : (j + 1) * 2 * C]
    spectral = total[:, 0:C] + total[:, C:]
    field = half_gelu(0.5 * (spectral + linear[...]))
    field = jnp.concatenate([field, jnp.zeros_like(field)], axis=1)
    out[...] = field.astype(BF).reshape(out.shape)


WIDE_BUFFER = (WIDE, SLOTS, 2 * C)
NARROW_BUFFER = (NARROW, YL, XL * KZ * 2 * C)
WIDTH = XL * KZ * 2 * C

NETWORK = (("in_w", (6, H), BF), ("in_b", (1, H), F32), ("mid_w", (H, H), BF), ("mid_b", (1, H), F32), ("out_w", (C, H), BF))
INPUTS = (
    ("owner", (1, BLKS), jnp.int32),
    ("cell", (1, BLKS), jnp.int32),
    ("fill", (1, BLKS), jnp.int32),
    ("feats", (C, PTS), BF),
    ("point_proj", (C, C), BF),
    *(("enc_" + name, shape, kind) for name, shape, kind in NETWORK),
    ("offsets", (3, BLKS * ROWS), F32),
    ("points", (BLKS, ROWS), jnp.int32),
    *(("dec_" + name, shape, kind) for name, shape, kind in NETWORK),
    ("cell_proj", (C, C), BF),
    ("skip", (C, C), F32),
    ("skip_b", (1, C), F32),
    ("table_z", (G, M * 2 * C), BF),
    ("forward_y", (2 * M, G), BF),
    ("forward_x", (4 * M * KZ, G * KZ), BF),
    ("inverse_x", (2 * G * KZ, 2 * M * KZ), BF),
    ("inverse_y", (2 * G, M), BF),
    ("spectral", (M, KZ, C, 2 * C), F32),
)
LAYERS = (("turned_w", (H, H), F32), ("first", (H, H), BF), ("second", (H, H), BF), ("second_b", (H, ROWS), F32))
SCRATCH = (
    ("sent", WIDE_BUFFER, BF),
    ("entries", WIDE_BUFFER, BF),
    ("pencils", NARROW_BUFFER, BF),
    ("columns", NARROW_BUFFER, BF),
    ("y_modes", WIDE_BUFFER, BF),
    ("slabs", WIDE_BUFFER, BF),
    ("mixed", WIDE_BUFFER, BF),
    ("rows", WIDE_BUFFER, BF),
    ("grid", NARROW_BUFFER, BF),
    ("spectra", NARROW_BUFFER, BF),
    ("reply", WIDE_BUFFER, BF),
    ("returned", WIDE_BUFFER, BF),
    ("work", (M * XL * KZ, 2 * C), F32),
    ("latent", (ENTRIES, 2 * C), F32),
    ("linear", (ENTRIES, C), F32),
    ("phases", (ENTRIES, M * 2 * C), BF),
    ("left", (M * 2 * KZ, KZ * C), F32),
    ("product", (M * 2 * KZ, 2 * C), F32),
    ("mixer", (M, KZ * C, 2 * C), BF),
    ("grouped", (HIGH * C, LOW), BF),
    ("sums", (BLKS, 2 * C), F32),
    ("blocks", (BLKS, 2 * C), F32),
    ("features", (16, LANES), F32),
    *(("enc_" + name, shape, kind) for name, shape, kind in LAYERS),
    *(("dec_" + name, shape, kind) for name, shape, kind in LAYERS),
    ("weights", (STEPS, C, LANES), F32),
    ("gathered", (BLKS, C), F32),
    ("totals", (HIGH * C + 16, LOW), F32),
)
NAMES = [name for name, _, _ in INPUTS]


def whole_body(*refs):
    count = len(INPUTS)
    source = dict(zip(NAMES, refs[:count]))
    out = refs[count]
    v = dict(zip(NAMES + [name for name, _, _ in SCRATCH], refs[count + 1 :]))
    in_sem, wide_send, wide_recv, narrow_send, narrow_recv = refs[-5:]
    copies = {
        name: pltpu.make_async_copy(source[name], v[name], in_sem.at[i]) for i, name in enumerate(NAMES)
    }
    for one in copies.values():
        one.start()
    all_in = greet()

    def need(*names):
        for name in names:
            copies[name].wait()

    def layers(net):
        need(*(net + name for name, _, _ in NETWORK))
        prepare_network(
            *(v[net + name] for name in ("in_w", "in_b", "mid_w", "mid_b", "turned_w", "first", "second", "second_b"))
        )
        return v[net + "first"], v[net + "second"], v[net + "second_b"], v[net + "out_w"]

    need("owner", "cell", "fill")
    prepare_blocks(v["owner"], v["cell"], v["fill"], v["blocks"])
    v["sums"][...] = v["blocks"][...]
    encoder = layers("enc_")
    need("feats", "point_proj")
    project_points(v["point_proj"], v["feats"], v["grouped"])
    need("offsets", "points")

    def encode(step, carry):
        encode_chunk(
            step, v["offsets"], v["points"], v["blocks"], v["features"], v["grouped"], encoder, v["sums"]
        )
        return carry

    lax.fori_loop(0, STEPS, encode, 0)
    pack_sums(v["owner"], v["blocks"], v["sums"], v["sent"])
    all_in()
    sends = []

    def move(axis, number, source_name, target_name, meanwhile=lambda: None):
        sizes = {"wide": (WIDE, wide_send, wide_recv), "narrow": (NARROW, narrow_send, narrow_recv)}
        size, send_sem, recv_sem = sizes[axis]
        start, receive, finish = exchange(
            axis, size, v[source_name], v[target_name], send_sem.at[number], recv_sem.at[number]
        )
        start()
        sends.append(finish)
        meanwhile()
        receive()

    def weigh(low, high):
        def step_body(step, carry):
            inputs, _ = chunk_inputs(step, v["offsets"], v["blocks"], v["features"])
            v["weights"][step] = network(*decoder, inputs)
            return carry

        lax.fori_loop(low, high, step_body, 0)

    decoder = layers("dec_")
    need("table_z", "forward_y", "forward_x", "inverse_x", "inverse_y", "spectral", "skip", "skip_b", "cell_proj")

    def beside_entries():
        weigh(0, STEPS // 2)

    def beside_pencils():
        linear = jnp.dot(
            v["latent"][:, 0:C], v["skip"][...], precision=lax.Precision.HIGHEST, preferred_element_type=F32
        )
        v["linear"][...] = linear + v["skip_b"][...]
        weigh(STEPS // 2, STEPS)

    def beside_columns():
        v["mixer"][...] = v["spectral"][...].reshape(M, KZ * C, 2 * C).astype(BF)
        entry_phases(v["entries"], v["table_z"], v["phases"])
        v["totals"][...] = jnp.zeros_like(v["totals"])

    move("wide", 0, "sent", "entries", beside_entries)
    forward_z(v["entries"], v["table_z"], v["pencils"], v["latent"])
    move("narrow", 0, "pencils", "columns", beside_pencils)
    forward_y(v["columns"], v["forward_y"], v["y_modes"], v["work"])
    move("wide", 1, "y_modes", "slabs", beside_columns)
    mix_x(v["slabs"], v["forward_x"], v["inverse_x"], v["mixer"], v["mixed"], v["left"], v["product"])
    move("wide", 2, "mixed", "rows")
    inverse_y(v["rows"], v["inverse_y"], v["grid"], v["work"])
    move("narrow", 1, "grid", "spectra")
    inverse_z(v["entries"], v["linear"], v["spectra"], v["phases"], v["reply"])
    move("wide", 3, "reply", "returned")
    unpack_values(v["owner"], v["blocks"], v["returned"], v["cell_proj"], v["gathered"])

    def decode(step, carry):
        decode_chunk(step, v["points"], v["blocks"], v["weights"], v["gathered"], v["totals"])
        return carry

    lax.fori_loop(0, STEPS, decode, 0)
    finish_points(v["totals"], out)
    for finish in sends:
        finish()


def whole_call():
    return pl.pallas_call(
        whole_body,
        out_shape=jax.ShapeDtypeStruct((C, PTS), BF),
        in_specs=[pl.BlockSpec(memory_space=pl.ANY)] * len(INPUTS),
        out_specs=pl.BlockSpec(memory_space=pltpu.VMEM),
        scratch_shapes=[pltpu.VMEM(shape, kind) for _, shape, kind in INPUTS + SCRATCH]
        + [
            pltpu.SemaphoreType.DMA((len(INPUTS),)),
            pltpu.SemaphoreType.DMA((4, WIDE)),
            pltpu.SemaphoreType.DMA((4, WIDE)),
            pltpu.SemaphoreType.DMA((2, NARROW)),
            pltpu.SemaphoreType.DMA((2, NARROW)),
        ],
        compiler_params=pltpu.CompilerParams(
            collective_id=0, has_side_effects=True, vmem_limit_bytes=60 * 1024 * 1024
        ),
        name="whole",
    )


def shards(
    point_feats,
    edge_offset,
    edge_point,
    block_fill,
    block_owner,
    block_cell,
    enc_in_w,
    enc_in_b,
    enc_mid_w,
    enc_mid_b,
    enc_out_w,
    point_proj,
    dec_in_w,
    dec_in_b,
    dec_mid_w,
    dec_mid_b,
    dec_out_w,
    cell_proj,
    skip_weight,
    skip_bias,
    spectral_weight,
):
    tables = (z_table(), y_forward_table(), x_forward_table(), x_inverse_table(), y_inverse_table())
    return whole_call()(
        block_owner.reshape(1, BLKS),
        block_cell[None, :],
        block_fill[None, :],
        point_feats,
        point_proj,
        enc_in_w.T,
        enc_in_b[None, :],
        enc_mid_w,
        enc_mid_b[None, :],
        enc_out_w,
        edge_offset,
        edge_point,
        dec_in_w.T,
        dec_in_b[None, :],
        dec_mid_w,
        dec_mid_b[None, :],
        dec_out_w,
        cell_proj,
        skip_weight,
        skip_bias[None, :],
        *[jnp.asarray(table) for table in tables],
        spectral_weight[0],
    )


def solution(mesh):
    return jax.shard_map(
        shards,
        mesh=mesh,
        in_specs=(
            P(None, ("wide", "narrow")),
            P(None, ("wide", "narrow")),
            P(("wide", "narrow"), None),
            P(("wide", "narrow")),
            P(("wide", "narrow"), None),
            P(("wide", "narrow")),
            P(),
            P(),
            P(),
            P(),
            P(),
            P(),
            P(),
            P(),
            P(),
            P(),
            P(),
            P(),
            P(),
            P(),
            P("wide", None, "narrow", None, None),
        ),
        out_specs=P(None, ("wide", "narrow")),
        check_vma=False,
    )
```

```python
import math
import types

import jax
import jax.numpy as jnp
import numpy as np
from jax import lax
from jax.experimental import pallas as pl
from jax.experimental.pallas import tpu as pltpu
from jax.sharding import PartitionSpec as P

G = 128
M = 32
C = 64
H = 128
ROWS = 128
WIDE = 32
NARROW = 8
SLOTS = 16
ENTRIES = WIDE * SLOTS
XL = G // WIDE
YL = G // NARROW
KZ = M // NARROW
PTS = 2048
BLKS = 256
LOW = 256
HIGH = PTS // LOW
STEP_BLKS = 32
LANES = STEP_BLKS * ROWS
STEPS = BLKS // STEP_BLKS
BF = jnp.bfloat16
F32 = jnp.float32

NT = (((1,), (1,)), ((), ()))
TN = (((0,), (0,)), ((), ()))


def dot(left, right, dims=(((1,), (0,)), ((), ()))):
    return lax.dot_general(left, right, dims, preferred_element_type=F32)


def angles(positions, waves):
    return 2.0 * np.pi * (np.outer(positions, waves) % G) / G


WAVES = np.arange(M) - M // 2


def z_table():
    turn = angles(np.arange(G), WAVES)
    both = np.stack([np.cos(turn), -np.sin(turn)], axis=2)
    return np.repeat(both.reshape(G, 2 * M), C, axis=1).astype(BF)


def y_forward_table():
    turn = angles(WAVES, np.arange(G))
    return np.concatenate([np.cos(turn), np.sin(turn)], axis=0).astype(BF)


def y_inverse_table():
    turn = angles(np.arange(G), WAVES)
    return np.concatenate([np.cos(turn), np.sin(turn)], axis=0).astype(BF)


def x_forward_table():
    turn = angles(WAVES, np.arange(G))
    same = np.eye(KZ)
    halves = []
    for wave in (np.cos(turn), np.sin(turn)):
        full = np.einsum("ix,kl->ikxl", wave, same)
        full = np.repeat(full[:, None], 2, axis=1)
        halves.append(full.reshape(M * 2 * KZ, G * KZ))
    return np.concatenate(halves, axis=0).astype(BF)


def x_inverse_table():
    turn = angles(np.arange(G), WAVES)
    same = np.eye(KZ)
    cos, sin = np.cos(turn) / M**3, np.sin(turn) / M**3
    halves = []
    for first, second in ((cos, -sin), (sin, cos)):
        full = np.einsum("xis,kl->xkisl", np.stack([first, second], axis=2), same)
        halves.append(full.reshape(G * KZ, M * 2 * KZ))
    return np.concatenate(halves, axis=0).astype(BF)


def half_gelu(half):
    slope = math.sqrt(2.0 / math.pi)
    inner = half * (half * half * (8.0 * slope * 0.044715) + 2.0 * slope)
    return half + half * jnp.tanh(inner)


def half_gelu_short(half):
    slope = math.sqrt(2.0 / math.pi)
    half = half.astype(BF)
    cubic, linear = jnp.full((), 8.0 * slope * 0.044715, BF), jnp.full((), 2.0 * slope, BF)
    return half + half * jnp.tanh(half * (half * half * cubic + linear))


def turned(value):
    lane = lax.broadcasted_iota(jnp.int32, value.shape, 1)
    rolled = pltpu.roll(value, C, 1)
    return jnp.where(lane < C, -rolled, rolled)


def prepare_network(in_w, in_b, mid_w, mid_b, turned_w, first, second, second_b):
    bias = 0.5 * in_b[...]
    high = bias.astype(BF).astype(F32)
    number = lax.broadcasted_iota(jnp.int32, (H, H), 0)
    turned_w[...] = jnp.where(number == 6, high, jnp.where(number == 7, bias - high, 0.0))
    turned_w[0:6, :] = 0.5 * in_w[...].astype(F32)
    first[...] = turned_w[...].T.astype(BF)
    second[...] = (0.5 * mid_w[...].astype(F32)).astype(BF)
    second_b[...] = jnp.broadcast_to(0.5 * mid_b[...], (H, H)).T


def network(first, second, second_b, third_w, features):
    hidden = half_gelu(dot(first[:, 0:16], features)).astype(BF)
    bias = jnp.concatenate([second_b[...]] * (features.shape[1] // ROWS), axis=1)
    hidden = half_gelu(dot(second[...], hidden) + bias).astype(BF)
    return dot(third_w[...], hidden)


FILL, OWNER, META = 8, 9, C


def prepare_blocks(owner, cell, fill, blocks):
    cell_row, cell_z = cell[...] >> 7, cell[...] & (G - 1)
    coord_x = owner[...] * XL + (cell_row >> 4)
    coord_y = lax.axis_index("narrow") * YL + (cell_row & (YL - 1))
    number = lax.broadcasted_iota(jnp.int32, (2 * C, BLKS), 0)
    facts = jnp.where((number == 6) | (number == 7), 1.0, 0.0)
    rows = [(3 + i, (2.0 * at.astype(F32) + 1.0) / G - 1.0) for i, at in enumerate((coord_x, coord_y, cell_z))]
    rows += [(FILL, fill[...]), (OWNER, owner[...]), (META, cell_row), (META + 1, cell_z), (META + 2, fill[...])]
    for place, value in rows:
        facts = jnp.where(number == place, value.astype(F32), facts)
    blocks[...] = facts.T


def block_lanes():
    lane = lax.broadcasted_iota(jnp.int32, (STEP_BLKS, LANES), 1)
    return lane - lax.broadcasted_iota(jnp.int32, (STEP_BLKS, LANES), 0) * ROWS


def edge_features(offsets, facts, distance, features_ref):
    inside = jnp.where((distance >= 0) & (distance < ROWS), 1.0, 0.0).astype(BF)
    features_ref[...] = dot(facts[:, 0:16].astype(BF), inside, TN)
    features_ref[0:3, :] = offsets
    return features_ref[...].astype(BF)


def live_lanes(facts, distance):
    fill = facts[:, FILL : FILL + 1].astype(jnp.int32)
    return jnp.where((distance >= 0) & (distance < fill), 1.0, 0.0)


def chunk(step):
    return pl.ds(pl.multiple_of(step * STEP_BLKS, STEP_BLKS), STEP_BLKS)


def point_row(points):
    return jnp.concatenate([points[i : i + 1, :] for i in range(STEP_BLKS)], axis=1)


def low_onehot(row):
    low = jnp.broadcast_to((row & (LOW - 1)).astype(F32), (16, LANES)).astype(BF)
    low = jnp.concatenate([low] * (LOW // 16), axis=0)
    number = lax.broadcasted_iota(jnp.int32, (LOW, LANES), 0).astype(F32).astype(BF)
    return jnp.where(low == number, jnp.ones((), BF), jnp.zeros((), BF))


def project_points(proj, feats, grouped):
    projected = dot(proj[...], feats[...]).astype(BF)
    for high in range(HIGH):
        grouped[high * C : (high + 1) * C, :] = projected[:, high * LOW : (high + 1) * LOW]


def chunk_inputs(step, offsets, blocks, features):
    facts = blocks[chunk(step), :]
    distance = block_lanes()
    lanes = pl.ds(pl.multiple_of(step * LANES, LANES), LANES)
    return edge_features(offsets[:, lanes], facts, distance, features), live_lanes(facts, distance)


PIECES = 16
PIECE = LANES // PIECES


def pick_high(spread, high_row):
    high_row = jnp.broadcast_to(high_row, (C, high_row.shape[1]))
    picked = spread[0:C]
    for high in range(1, HIGH):
        picked = jnp.where(high_row == high, spread[high * C : (high + 1) * C], picked)
    return picked


def encode_chunk(step, offsets, points, blocks, features, grouped, layers, sums):
    first, second, second_b, third = layers
    row = point_row(points[chunk(step), :])
    high_row = row >> 8
    onehot = low_onehot(row)
    inputs, live = chunk_inputs(step, offsets, blocks, features)
    bias = jnp.concatenate([second_b[...]] * (PIECE // ROWS), axis=1)
    raw, hidden, deep, weight, spread, message = {}, {}, {}, {}, {}, {}
    for tick in range(PIECES + 5):
        at = [tick - age if 0 <= tick - age < PIECES else None for age in range(6)]
        lanes = [None if piece is None else slice(piece * PIECE, (piece + 1) * PIECE) for piece in at]
        if at[1] is not None:
            hidden[at[1]] = half_gelu_short(raw.pop(at[1]))
        if at[3] is not None:
            deep[at[3]] = half_gelu_short(deep[at[3]] + bias)
        if at[5] is not None:
            picked = pick_high(spread.pop(at[5]), high_row[:, lanes[5]])
            message[at[5]] = (weight.pop(at[5]) * picked).astype(BF)
        if at[0] is not None:
            raw[at[0]] = dot(first[:, 0:16], inputs[:, lanes[0]])
        if at[2] is not None:
            deep[at[2]] = dot(second[...], hidden.pop(at[2]))
        if at[4] is not None:
            weight[at[4]] = dot(third[...], deep.pop(at[4]))
            spread[at[4]] = dot(grouped[...], onehot[:, lanes[4]])
    messages = jnp.concatenate([message[piece] for piece in range(PIECES)], axis=1)
    sums[chunk(step), 0:C] = dot(live.astype(BF), messages, NT)


def make_placer(owner, blocks, placer):
    before = lax.broadcasted_iota(jnp.int32, (BLKS, BLKS), 0) < lax.broadcasted_iota(
        jnp.int32, (BLKS, BLKS), 1
    )
    same = blocks[:, OWNER : OWNER + 1].astype(jnp.int32) == owner[...]
    rank = jnp.sum(jnp.where(same & before, 1, 0), axis=0, keepdims=True)
    target = owner[...] * SLOTS + rank
    slot = lax.broadcasted_iota(jnp.int32, (ENTRIES, BLKS), 0)
    placer[...] = jnp.where(slot == target, 1.0, 0.0).astype(BF)


def make_picker(owner, blocks, picker):
    before = lax.broadcasted_iota(jnp.int32, (BLKS, BLKS), 1) < lax.broadcasted_iota(
        jnp.int32, (BLKS, BLKS), 0
    )
    own = blocks[:, OWNER : OWNER + 1].astype(jnp.int32)
    rank = jnp.sum(jnp.where((own == owner[...]) & before, 1, 0), axis=1, keepdims=True)
    target = own * SLOTS + rank
    slot = lax.broadcasted_iota(jnp.int32, (BLKS, ENTRIES), 1)
    picker[...] = jnp.where(slot == target, 1.0, 0.0).astype(BF)


def unpack_values(picker, returned, proj, gathered):
    values = dot(picker[...], returned[...].reshape(ENTRIES, 2 * C)).astype(BF)
    gathered[...] = dot(values[:, 0:C], proj[...], NT)


def decode_chunk(step, points, blocks, weights, gathered, totals):
    live = live_lanes(blocks[chunk(step), :], block_lanes())
    alive = jnp.sum(live, axis=0, keepdims=True)
    live = live.astype(BF)
    cells = gathered[chunk(step), :]
    cells_high = cells.astype(BF)
    cells_low = (cells - cells_high.astype(F32)).astype(BF)
    pieces = jnp.concatenate([cells_high, cells_low], axis=0)
    spread = dot(pieces, jnp.concatenate([live, live], axis=0), TN)
    message = (weights[step] * spread).astype(BF)
    row = point_row(points[chunk(step), :])
    high = jnp.broadcast_to((row >> 8).astype(F32), (16, LANES)).astype(BF)
    high_rows = jnp.concatenate([high] * (C // 16), axis=0)
    parts = [jnp.where(high_rows == jnp.full((), i, BF), message, jnp.zeros((), BF)) for i in range(HIGH)]
    number = lax.broadcasted_iota(jnp.int32, (16, LANES), 0)
    count = jnp.where(number == row >> 8, jnp.broadcast_to(alive, (16, LANES)), 0.0)
    parts.append(count.astype(BF))
    totals[...] += dot(jnp.concatenate(parts, axis=0), low_onehot(row), NT)


def finish_points(totals, out):
    for high in range(HIGH):
        degree = totals[HIGH * C + high : HIGH * C + high + 1, :]
        scale = 1.0 / jnp.maximum(jnp.sqrt(degree), 1.0)
        value = totals[high * C : (high + 1) * C, :] * scale
        out[:, high * LOW : (high + 1) * LOW] = value.astype(BF)


def entry_cells(received):
    cell_row = received[:, C : C + 1].astype(F32)
    cell_z = received[:, C + 1 : C + 2].astype(F32)
    lane = lax.broadcasted_iota(jnp.int32, (16, 2 * C), 1)
    sub = lax.broadcasted_iota(jnp.int32, (16, 2 * C), 0)
    picker = jnp.where(lane == sub + C, 1.0, 0.0).astype(BF)
    rows = dot(picker, received, NT)
    return cell_row, cell_z, rows[0:1, :], rows[1:2, :]


def exchange(axis, count, source, target, send_sem, recv_sem):
    me = lax.axis_index(axis)

    def copy(ahead, peer):
        return pltpu.make_async_remote_copy(
            src_ref=source.at[peer],
            dst_ref=target.at[me],
            send_sem=send_sem.at[ahead],
            recv_sem=recv_sem.at[ahead],
            device_id={axis: peer},
            device_id_type=pl.DeviceIdType.MESH,
        )

    def each(action):
        def step(ahead, carry):
            action(copy(ahead, lax.rem(me + ahead, count)))
            return carry

        lax.fori_loop(1, count, step, 0)

    def start(ahead):
        copy(ahead, lax.rem(me + ahead, count)).start()

    def start_all():
        each(lambda one: one.start())
        target[me] = source[me]

    return start, start_all, lambda: each(lambda one: one.wait_recv()), lambda: each(lambda one: one.wait_send())


def greet():
    barrier = pltpu.get_barrier_semaphore()
    for axis, count in (("wide", WIDE), ("narrow", NARROW)):
        me = lax.axis_index(axis)

        def step(ahead, carry):
            pl.semaphore_signal(
                barrier,
                inc=1,
                device_id={axis: lax.rem(me + ahead, count)},
                device_id_type=pl.DeviceIdType.MESH,
            )
            return carry

        lax.fori_loop(1, count, step, 0)
    return lambda: pl.semaphore_wait(barrier, WIDE + NARROW - 2)


def entry_phases(received_ref, table, phases):
    cell_z = received_ref[...].reshape(ENTRIES, 2 * C)[:, C + 1 : C + 2].astype(F32)
    position = lax.broadcasted_iota(jnp.int32, (ENTRIES, G), 1).astype(F32)
    at_z = jnp.where(position == cell_z, 1.0, 0.0).astype(BF)
    phases[...] = dot(at_z, table[...]).astype(BF)


def forward_z(received_ref, table, out, own_out, latent, start):
    received = received_ref[...].reshape(ENTRIES, 2 * C)
    cell_row, cell_z, row_xy, row_z = entry_cells(received)
    same = (cell_row * G + cell_z) == (row_xy * G + row_z)
    totals = dot(jnp.where(same, 1.0, 0.0).astype(BF), received)
    scale = 1.0 / jnp.maximum(jnp.sqrt(totals[:, C + 2 : C + 3]), 1.0)
    latent[...] = totals * scale
    own = received.astype(F32) * scale
    lane = lax.broadcasted_iota(jnp.int32, own.shape, 1)
    own = jnp.where(lane < C, own, pltpu.roll(own, C, 1))
    position = lax.broadcasted_iota(jnp.int32, (ENTRIES, G), 1).astype(F32)
    at_z = jnp.where(position == cell_z, 1.0, 0.0).astype(BF)
    pencil = lax.broadcasted_iota(jnp.int32, (XL * YL, ENTRIES), 0).astype(F32)
    at_row = jnp.where(pencil == row_xy, 1.0, 0.0).astype(BF)
    width = KZ * 2 * C
    spread = jnp.concatenate([own] * KZ, axis=1)
    me = lax.axis_index("narrow")
    for ahead in range(1, NARROW + 1):
        group = lax.rem(me + ahead, NARROW)
        phases = dot(at_z, table[:, pl.ds(pl.multiple_of(group * width, width), width)])
        modes = dot(at_row, (spread * phases).astype(BF)).astype(BF)
        place = out if ahead < NARROW else own_out
        for x in range(XL):
            place[group, :, x * width : (x + 1) * width] = modes[x * YL : (x + 1) * YL, :]
        if ahead < NARROW:
            start(ahead)


def forward_y(received, table, out, columns):
    both = dot(table[...], received[...].reshape(G, XL * KZ * 2 * C))
    for j in range(XL * KZ):
        lanes = slice(j * 2 * C, (j + 1) * 2 * C)
        columns[pl.ds(j, M, stride=XL * KZ), :] = both[0:M, lanes] - turned(both[M:, lanes])
    out[...] = columns[...].astype(BF).reshape(out.shape)


def mix_x(received, forward, inverse, weight, out, left, product):
    count = M * 2 * KZ
    both = dot(forward[...], received[...].reshape(G * KZ, 2 * C))
    modes = both[0:count] - turned(both[count:])
    row = lax.broadcasted_iota(jnp.int32, (count, 2 * C), 0)
    lane = lax.broadcasted_iota(jnp.int32, (count, 2 * C), 1)
    real_row = (row // KZ) % 2 == 0
    wide = jnp.where(real_row == (lane < C), modes, pltpu.roll(modes, C, 1))
    for half in range(KZ // 2):
        keep = row % KZ == 2 * half + lane // C
        left[:, half * 2 * C : (half + 1) * 2 * C] = jnp.where(keep, wide, 0.0)
    for kx in range(M):
        rows = slice(kx * 2 * KZ, (kx + 1) * 2 * KZ)
        product[rows, :] = dot(left[rows, :].astype(BF), weight[kx])
    back = dot(inverse[...], product[...].astype(BF))
    cells = G * KZ
    out[...] = (back[0:cells] + turned(back[cells:])).astype(BF).reshape(out.shape)


def inverse_y(received, table, out, columns):
    columns[...] = received[...].reshape(M * XL * KZ, 2 * C).astype(F32)
    for j in range(XL * KZ):
        column = columns[pl.ds(j, M, stride=XL * KZ), :].astype(BF)
        both = dot(table[...], column)
        value = both[0:G] + turned(both[G:])
        out[:, :, j * 2 * C : (j + 1) * 2 * C] = value.astype(BF).reshape(NARROW, YL, 2 * C)


def inverse_z(received_ref, linear, spectra, phases, out):
    cell_row = received_ref[...].reshape(ENTRIES, 2 * C)[:, C : C + 1].astype(F32)
    pencil = lax.broadcasted_iota(jnp.int32, (ENTRIES, XL * YL), 1).astype(F32)
    at_row = jnp.where(pencil == cell_row, 1.0, 0.0).astype(BF)
    width = KZ * 2 * C
    total = jnp.zeros((ENTRIES, 2 * C), F32)
    for group in range(NARROW):
        pencils = jnp.concatenate(
            [spectra[group, :, x * width : (x + 1) * width] for x in range(XL)], axis=0
        )
        terms = phases[:, group * width : (group + 1) * width].astype(F32) * dot(at_row, pencils)
        for j in range(KZ):
            total += terms[:, j * 2 * C : (j + 1) * 2 * C]
    spectral = total[:, 0:C] + total[:, C:]
    field = half_gelu(0.5 * (spectral + linear[...]))
    field = jnp.concatenate([field, jnp.zeros_like(field)], axis=1)
    out[...] = field.astype(BF).reshape(out.shape)


WIDE_BUFFER = (WIDE, SLOTS, 2 * C)
NARROW_BUFFER = (NARROW, YL, XL * KZ * 2 * C)
WIDTH = XL * KZ * 2 * C

I32 = jnp.int32
NETWORK = dict(in_w=((6, H), BF), in_b=((1, H), F32), mid_w=((H, H), BF), mid_b=((1, H), F32), out_w=((C, H), BF))
LAYERS = dict(turned_w=((H, H), F32), first=((H, H), BF), second=((H, H), BF), second_b=((H, ROWS), F32))
BLOCK_INPUTS = dict(
    owner=((1, BLKS), I32),
    cell=((1, BLKS), I32),
    fill=((1, BLKS), I32),
    feats=((C, PTS), BF),
    point_proj=((C, C), BF),
)
EDGE_INPUTS = dict(offsets=((3, BLKS * ROWS), F32), points=((BLKS, ROWS), I32))
GRID_INPUTS = dict(
    cell_proj=((C, C), BF),
    skip=((C, C), F32),
    skip_b=((1, C), F32),
    table_z=((G, M * 2 * C), BF),
    forward_y=((2 * M, G), BF),
    forward_x=((4 * M * KZ, G * KZ), BF),
    inverse_x=((2 * G * KZ, 2 * M * KZ), BF),
    inverse_y=((2 * G, M), BF),
    spectral=((M, KZ, C, 2 * C), F32),
)
SCRATCH = dict(
    sent=(WIDE_BUFFER, BF),
    entries=(WIDE_BUFFER, BF),
    pencils=(NARROW_BUFFER, BF),
    columns=(NARROW_BUFFER, BF),
    y_modes=(WIDE_BUFFER, BF),
    slabs=(WIDE_BUFFER, BF),
    mixed=(WIDE_BUFFER, BF),
    rows=(WIDE_BUFFER, BF),
    grid=(NARROW_BUFFER, BF),
    spectra=(NARROW_BUFFER, BF),
    reply=(WIDE_BUFFER, BF),
    returned=(WIDE_BUFFER, BF),
    work=((M * XL * KZ, 2 * C), F32),
    latent=((ENTRIES, 2 * C), F32),
    linear=((ENTRIES, C), F32),
    phases=((ENTRIES, M * 2 * C), BF),
    left=((M * 2 * KZ, KZ * C), F32),
    product=((M * 2 * KZ, 2 * C), F32),
    mixer=((M, KZ * C, 2 * C), BF),
    grouped=((HIGH * C, LOW), BF),
    sums=((BLKS, 2 * C), F32),
    blocks=((BLKS, 2 * C), F32),
    placer=((ENTRIES, BLKS), BF),
    picker=((BLKS, ENTRIES), BF),
    features=((16, LANES), F32),
    weights=((STEPS, C, LANES), F32),
    gathered=((BLKS, C), F32),
    totals=((HIGH * C + 16, LOW), F32),
)
INPUT_GROUPS = (BLOCK_INPUTS, NETWORK, EDGE_INPUTS, NETWORK, GRID_INPUTS)
INPUTS = [item for group in INPUT_GROUPS for item in group.values()]
SCRATCH_GROUPS = INPUT_GROUPS + (LAYERS, LAYERS, SCRATCH)


def whole_body(*refs):
    count = len(INPUTS)
    out = refs[count]
    in_sem, wide_send, wide_recv, narrow_send, narrow_recv = refs[-5:]
    rest = iter(refs[count + 1 : -5])
    held = [types.SimpleNamespace(**{name: next(rest) for name in group}) for group in SCRATCH_GROUPS]
    block, enc, edge, dec, grid, enc_layers, dec_layers, v = held
    places = refs[count + 1 : 2 * count + 1]
    copies = [pltpu.make_async_copy(refs[i], places[i], in_sem.at[i]) for i in range(count)]
    for one in copies:
        one.start()
    all_in = greet()
    ends = np.cumsum([len(group) for group in INPUT_GROUPS])

    def need(low, high):
        for one in copies[low:high]:
            one.wait()

    def layers(raw, made):
        prepare_network(
            raw.in_w, raw.in_b, raw.mid_w, raw.mid_b, made.turned_w, made.first, made.second, made.second_b
        )
        return made.first, made.second, made.second_b, raw.out_w

    need(0, ends[1])
    prepare_blocks(block.owner, block.cell, block.fill, v.blocks)
    v.sums[...] = v.blocks[...]
    encoder = layers(enc, enc_layers)
    project_points(block.point_proj, block.feats, v.grouped)
    make_placer(block.owner, v.blocks, v.placer)
    need(ends[1], ends[2])

    def encode(step, carry):
        encode_chunk(step, edge.offsets, edge.points, v.blocks, v.features, v.grouped, encoder, v.sums)
        return carry

    lax.fori_loop(0, STEPS, encode, 0)
    v.sent[...] = dot(v.placer[...], v.sums[...].astype(BF)).astype(BF).reshape(v.sent.shape)
    all_in()

    def wide(number, source, target):
        return exchange("wide", WIDE, source, target, wide_send.at[number], wide_recv.at[number])

    def narrow(number, source, target):
        return exchange("narrow", NARROW, source, target, narrow_send.at[number], narrow_recv.at[number])

    _, start, receive, finish_entries = wide(0, v.sent, v.entries)
    start()
    need(ends[2], ends[4])
    decoder = layers(dec, dec_layers)

    def weigh(low, high):
        def step_body(step, carry):
            inputs, _ = chunk_inputs(step, edge.offsets, v.blocks, v.features)
            v.weights[step] = network(*decoder, inputs)
            return carry

        lax.fori_loop(low, high, step_body, 0)

    weigh(0, 2)
    receive()

    start_one, _, receive, finish_pencils = narrow(0, v.pencils, v.columns)
    forward_z(v.entries, grid.table_z, v.pencils, v.columns, v.latent, start_one)
    finish_entries()
    linear = jnp.dot(
        v.latent[:, 0:C], grid.skip[...], precision=lax.Precision.HIGHEST, preferred_element_type=F32
    )
    v.linear[...] = linear + grid.skip_b[...]
    weigh(2, 4)
    receive()

    forward_y(v.columns, grid.forward_y, v.y_modes, v.work)
    _, start, receive, finish_modes = wide(1, v.y_modes, v.slabs)
    start()
    finish_pencils()
    v.mixer[...] = grid.spectral[...].reshape(M, KZ * C, 2 * C).astype(BF)
    weigh(4, 6)
    receive()

    mix_x(v.slabs, grid.forward_x, grid.inverse_x, v.mixer, v.mixed, v.left, v.product)
    _, start, receive, finish_mixed = wide(2, v.mixed, v.rows)
    start()
    finish_modes()
    entry_phases(v.entries, grid.table_z, v.phases)
    make_picker(block.owner, v.blocks, v.picker)
    weigh(6, 7)
    receive()

    inverse_y(v.rows, grid.inverse_y, v.grid, v.work)
    _, start, receive, finish_grid = narrow(1, v.grid, v.spectra)
    start()
    finish_mixed()
    weigh(7, STEPS)
    receive()

    inverse_z(v.entries, v.linear, v.spectra, v.phases, v.reply)
    _, start, receive, finish_reply = wide(3, v.reply, v.returned)
    start()
    finish_grid()
    v.totals[...] = jnp.zeros_like(v.totals)
    receive()
    unpack_values(v.picker, v.returned, grid.cell_proj, v.gathered)

    def decode(step, carry):
        decode_chunk(step, edge.points, v.blocks, v.weights, v.gathered, v.totals)
        return carry

    lax.fori_loop(0, STEPS, decode, 0)
    finish_points(v.totals, out)
    finish_reply()


def whole_call():
    scratch = [item for group in SCRATCH_GROUPS for item in group.values()]
    return pl.pallas_call(
        whole_body,
        out_shape=jax.ShapeDtypeStruct((C, PTS), BF),
        in_specs=[pl.BlockSpec(memory_space=pl.ANY)] * len(INPUTS),
        out_specs=pl.BlockSpec(memory_space=pltpu.VMEM),
        scratch_shapes=[pltpu.VMEM(shape, kind) for shape, kind in scratch]
        + [
            pltpu.SemaphoreType.DMA((len(INPUTS),)),
            pltpu.SemaphoreType.DMA((4, WIDE)),
            pltpu.SemaphoreType.DMA((4, WIDE)),
            pltpu.SemaphoreType.DMA((2, NARROW)),
            pltpu.SemaphoreType.DMA((2, NARROW)),
        ],
        compiler_params=pltpu.CompilerParams(
            collective_id=0, has_side_effects=True, vmem_limit_bytes=60 * 1024 * 1024
        ),
        name="whole",
    )


def shards(
    point_feats,
    edge_offset,
    edge_point,
    block_fill,
    block_owner,
    block_cell,
    enc_in_w,
    enc_in_b,
    enc_mid_w,
    enc_mid_b,
    enc_out_w,
    point_proj,
    dec_in_w,
    dec_in_b,
    dec_mid_w,
    dec_mid_b,
    dec_out_w,
    cell_proj,
    skip_weight,
    skip_bias,
    spectral_weight,
):
    tables = (z_table(), y_forward_table(), x_forward_table(), x_inverse_table(), y_inverse_table())
    return whole_call()(
        block_owner.reshape(1, BLKS),
        block_cell[None, :],
        block_fill[None, :],
        point_feats,
        point_proj,
        enc_in_w.T,
        enc_in_b[None, :],
        enc_mid_w,
        enc_mid_b[None, :],
        enc_out_w,
        edge_offset,
        edge_point,
        dec_in_w.T,
        dec_in_b[None, :],
        dec_mid_w,
        dec_mid_b[None, :],
        dec_out_w,
        cell_proj,
        skip_weight,
        skip_bias[None, :],
        *[jnp.asarray(table) for table in tables],
        spectral_weight[0],
    )


def solution(mesh):
    return jax.shard_map(
        shards,
        mesh=mesh,
        in_specs=(
            P(None, ("wide", "narrow")),
            P(None, ("wide", "narrow")),
            P(("wide", "narrow"), None),
            P(("wide", "narrow")),
            P(("wide", "narrow"), None),
            P(("wide", "narrow")),
            P(),
            P(),
            P(),
            P(),
            P(),
            P(),
            P(),
            P(),
            P(),
            P(),
            P(),
            P(),
            P(),
            P(),
            P("wide", None, "narrow", None, None),
        ),
        out_specs=P(None, ("wide", "narrow")),
        check_vma=False,
    )
```

```python
import math
import types

import jax
import jax.numpy as jnp
import numpy as np
from jax import lax
from jax.experimental import pallas as pl
from jax.experimental.pallas import tpu as pltpu
from jax.sharding import PartitionSpec as P

G = 128
M = 32
C = 64
H = 128
ROWS = 128
WIDE = 32
NARROW = 8
SLOTS = 16
ENTRIES = WIDE * SLOTS
XL = G // WIDE
YL = G // NARROW
KZ = M // NARROW
PTS = 2048
BLKS = 256
LOW = 256
HIGH = PTS // LOW
STEP_BLKS = 64
LANES = STEP_BLKS * ROWS
STEPS = BLKS // STEP_BLKS
BF = jnp.bfloat16
F32 = jnp.float32

NT = (((1,), (1,)), ((), ()))
TN = (((0,), (0,)), ((), ()))


def dot(left, right, dims=(((1,), (0,)), ((), ()))):
    return lax.dot_general(left, right, dims, preferred_element_type=F32)


def angles(positions, waves):
    return 2.0 * np.pi * (np.outer(positions, waves) % G) / G


WAVES = np.arange(M) - M // 2


def z_table():
    turn = angles(np.arange(G), WAVES)
    both = np.stack([np.cos(turn), -np.sin(turn)], axis=2)
    return np.repeat(both.reshape(G, 2 * M), C, axis=1).astype(BF)


def y_forward_table():
    turn = angles(WAVES, np.arange(G))
    return np.concatenate([np.cos(turn), np.sin(turn)], axis=0).astype(BF)


def y_inverse_table():
    turn = angles(np.arange(G), WAVES)
    return np.concatenate([np.cos(turn), np.sin(turn)], axis=0).astype(BF)


def x_forward_table():
    turn = angles(WAVES, np.arange(G))
    same = np.eye(KZ)
    halves = []
    for wave in (np.cos(turn), np.sin(turn)):
        full = np.einsum("ix,kl->ikxl", wave, same)
        full = np.repeat(full[:, None], 2, axis=1)
        halves.append(full.reshape(M * 2 * KZ, G * KZ))
    return np.concatenate(halves, axis=0).astype(BF)


def x_inverse_table():
    turn = angles(np.arange(G), WAVES)
    same = np.eye(KZ)
    cos, sin = np.cos(turn) / M**3, np.sin(turn) / M**3
    halves = []
    for first, second in ((cos, -sin), (sin, cos)):
        full = np.einsum("xis,kl->xkisl", np.stack([first, second], axis=2), same)
        halves.append(full.reshape(G * KZ, M * 2 * KZ))
    return np.concatenate(halves, axis=0).astype(BF)


def half_gelu(half):
    slope = math.sqrt(2.0 / math.pi)
    inner = half * (half * half * (8.0 * slope * 0.044715) + 2.0 * slope)
    return half + half * jnp.tanh(inner)


def turned(value):
    lane = lax.broadcasted_iota(jnp.int32, value.shape, 1)
    rolled = pltpu.roll(value, C, 1)
    return jnp.where(lane < C, -rolled, rolled)


def prepare_network(in_w, in_b, mid_w, mid_b, turned_w, first, second, second_b):
    bias = 0.5 * in_b[...]
    high = bias.astype(BF).astype(F32)
    number = lax.broadcasted_iota(jnp.int32, (H, H), 0)
    turned_w[...] = jnp.where(number == 6, high, jnp.where(number == 7, bias - high, 0.0))
    turned_w[0:6, :] = 0.5 * in_w[...].astype(F32)
    first[...] = turned_w[...].T.astype(BF)
    second[...] = (0.5 * mid_w[...].astype(F32)).astype(BF)
    second_b[...] = jnp.broadcast_to(0.5 * mid_b[...], (H, H)).T


def network(first, second, second_b, third_w, features):
    hidden = half_gelu(dot(first[:, 0:16], features)).astype(BF)
    bias = jnp.concatenate([second_b[...]] * (features.shape[1] // ROWS), axis=1)
    hidden = half_gelu(dot(second[...], hidden) + bias).astype(BF)
    return dot(third_w[...], hidden)


FILL, OWNER, META = 8, 9, C


def prepare_blocks(owner, cell, fill, blocks):
    cell_row, cell_z = cell[...] >> 7, cell[...] & (G - 1)
    coord_x = owner[...] * XL + (cell_row >> 4)
    coord_y = lax.axis_index("narrow") * YL + (cell_row & (YL - 1))
    number = lax.broadcasted_iota(jnp.int32, (2 * C, BLKS), 0)
    facts = jnp.where((number == 6) | (number == 7), 1.0, 0.0)
    rows = [(3 + i, (2.0 * at.astype(F32) + 1.0) / G - 1.0) for i, at in enumerate((coord_x, coord_y, cell_z))]
    rows += [(FILL, fill[...]), (OWNER, owner[...]), (META, cell_row), (META + 1, cell_z), (META + 2, fill[...])]
    for place, value in rows:
        facts = jnp.where(number == place, value.astype(F32), facts)
    blocks[...] = facts.T


def block_lanes():
    lane = lax.broadcasted_iota(jnp.int32, (STEP_BLKS, LANES), 1)
    return lane - lax.broadcasted_iota(jnp.int32, (STEP_BLKS, LANES), 0) * ROWS


def edge_features(offsets, facts, distance, features_ref):
    inside = jnp.where((distance >= 0) & (distance < ROWS), 1.0, 0.0).astype(BF)
    features_ref[...] = dot(facts[:, 0:16].astype(BF), inside, TN)
    features_ref[0:3, :] = offsets
    return features_ref[...].astype(BF)


def live_lanes(facts, distance):
    fill = facts[:, FILL : FILL + 1].astype(jnp.int32)
    return jnp.where((distance >= 0) & (distance < fill), 1.0, 0.0)


def chunk(step):
    return pl.ds(pl.multiple_of(step * STEP_BLKS, STEP_BLKS), STEP_BLKS)


def point_row(points):
    return jnp.concatenate([points[i : i + 1, :] for i in range(STEP_BLKS)], axis=1)


def low_onehot(row):
    low = jnp.broadcast_to((row & (LOW - 1)).astype(F32), (16, LANES)).astype(BF)
    low = jnp.concatenate([low] * (LOW // 16), axis=0)
    number = lax.broadcasted_iota(jnp.int32, (LOW, LANES), 0).astype(F32).astype(BF)
    return jnp.where(low == number, jnp.ones((), BF), jnp.zeros((), BF))


def project_points(proj, feats, grouped):
    projected = dot(proj[...], feats[...]).astype(BF)
    for high in range(HIGH):
        grouped[high * C : (high + 1) * C, :] = projected[:, high * LOW : (high + 1) * LOW]


def chunk_inputs(step, offsets, blocks, features):
    facts = blocks[chunk(step), :]
    distance = block_lanes()
    lanes = pl.ds(pl.multiple_of(step * LANES, LANES), LANES)
    return edge_features(offsets[:, lanes], facts, distance, features), live_lanes(facts, distance)


PIECES = 16
PIECE = LANES // PIECES


def pick_high(spread, high_row):
    high_row = jnp.broadcast_to(high_row, (C, high_row.shape[1]))
    picked = spread[0:C]
    for high in range(1, HIGH):
        picked = jnp.where(high_row == high, spread[high * C : (high + 1) * C], picked)
    return picked


def encode_chunk(step, offsets, points, blocks, features, grouped, layers, sums):
    first, second, second_b, third = layers
    row = point_row(points[chunk(step), :])
    high_row = row >> 8
    onehot = low_onehot(row)
    inputs, live = chunk_inputs(step, offsets, blocks, features)
    bias = jnp.concatenate([second_b[...]] * (PIECE // ROWS), axis=1)
    raw, hidden, deep, weight, spread, message = {}, {}, {}, {}, {}, {}
    for tick in range(PIECES + 5):
        at = [tick - age if 0 <= tick - age < PIECES else None for age in range(6)]
        lanes = [None if piece is None else slice(piece * PIECE, (piece + 1) * PIECE) for piece in at]
        if at[1] is not None:
            hidden[at[1]] = half_gelu(raw.pop(at[1])).astype(BF)
        if at[3] is not None:
            deep[at[3]] = half_gelu(deep[at[3]] + bias).astype(BF)
        if at[5] is not None:
            picked = pick_high(spread.pop(at[5]), high_row[:, lanes[5]])
            message[at[5]] = (weight.pop(at[5]) * picked).astype(BF)
        if at[0] is not None:
            raw[at[0]] = dot(first[:, 0:16], inputs[:, lanes[0]])
            spread[at[0]] = dot(grouped[...], onehot[:, lanes[0]])
        if at[2] is not None:
            deep[at[2]] = dot(second[...], hidden.pop(at[2]))
        if at[4] is not None:
            weight[at[4]] = dot(third[...], deep.pop(at[4]))
    messages = jnp.concatenate([message[piece] for piece in range(PIECES)], axis=1)
    sums[chunk(step), 0:C] = dot(live.astype(BF), messages, NT)


def make_placer(owner, blocks, placer):
    before = lax.broadcasted_iota(jnp.int32, (BLKS, BLKS), 0) < lax.broadcasted_iota(
        jnp.int32, (BLKS, BLKS), 1
    )
    same = blocks[:, OWNER : OWNER + 1].astype(jnp.int32) == owner[...]
    rank = jnp.sum(jnp.where(same & before, 1, 0), axis=0, keepdims=True)
    target = owner[...] * SLOTS + rank
    slot = lax.broadcasted_iota(jnp.int32, (ENTRIES, BLKS), 0)
    placer[...] = jnp.where(slot == target, 1.0, 0.0).astype(BF)


def make_picker(owner, blocks, picker):
    before = lax.broadcasted_iota(jnp.int32, (BLKS, BLKS), 1) < lax.broadcasted_iota(
        jnp.int32, (BLKS, BLKS), 0
    )
    own = blocks[:, OWNER : OWNER + 1].astype(jnp.int32)
    rank = jnp.sum(jnp.where((own == owner[...]) & before, 1, 0), axis=1, keepdims=True)
    target = own * SLOTS + rank
    slot = lax.broadcasted_iota(jnp.int32, (BLKS, ENTRIES), 1)
    picker[...] = jnp.where(slot == target, 1.0, 0.0).astype(BF)


def unpack_values(picker, returned, proj, gathered):
    values = dot(picker[...], returned[...].reshape(ENTRIES, 2 * C)).astype(BF)
    gathered[...] = dot(values[:, 0:C], proj[...], NT)


def decode_chunk(step, points, blocks, weights, gathered, totals):
    alive = jnp.sum(live_lanes(blocks[chunk(step), :], block_lanes()), axis=0, keepdims=True)
    cells = gathered[chunk(step), :]
    cells = jnp.concatenate([cells, cells], axis=1)
    cells = jnp.concatenate([cells] * (ROWS // STEP_BLKS), axis=0).T
    spread = jnp.concatenate(
        [jnp.broadcast_to(cells[0:C, i : i + 1], (C, ROWS)) for i in range(STEP_BLKS)], axis=1
    )
    message = (weights[step] * spread).astype(BF)
    row = jnp.where(alive > 0.5, point_row(points[chunk(step), :]), -1)
    high = jnp.broadcast_to((row >> 8).astype(F32), (16, LANES)).astype(BF)
    high_rows = jnp.concatenate([high] * (C // 16), axis=0)
    parts = [jnp.where(high_rows == jnp.full((), i, BF), message, jnp.zeros((), BF)) for i in range(HIGH)]
    number = lax.broadcasted_iota(jnp.int32, (16, LANES), 0)
    parts.append(jnp.where(number == row >> 8, 1.0, 0.0).astype(BF))
    totals[...] += dot(jnp.concatenate(parts, axis=0), low_onehot(row), NT)


def finish_points(totals, out):
    for high in range(HIGH):
        degree = totals[HIGH * C + high : HIGH * C + high + 1, :]
        scale = 1.0 / jnp.maximum(jnp.sqrt(degree), 1.0)
        value = totals[high * C : (high + 1) * C, :] * scale
        out[:, high * LOW : (high + 1) * LOW] = value.astype(BF)


def entry_cells(received):
    cell_row = received[:, C : C + 1].astype(F32)
    cell_z = received[:, C + 1 : C + 2].astype(F32)
    lane = lax.broadcasted_iota(jnp.int32, (16, 2 * C), 1)
    sub = lax.broadcasted_iota(jnp.int32, (16, 2 * C), 0)
    picker = jnp.where(lane == sub + C, 1.0, 0.0).astype(BF)
    rows = dot(picker, received, NT)
    return cell_row, cell_z, rows[0:1, :], rows[1:2, :]


def exchange(axis, count, source, target, send_sem, recv_sem):
    me = lax.axis_index(axis)

    def copy(ahead, peer):
        return pltpu.make_async_remote_copy(
            src_ref=source.at[peer],
            dst_ref=target.at[me],
            send_sem=send_sem.at[ahead],
            recv_sem=recv_sem.at[ahead],
            device_id={axis: peer},
            device_id_type=pl.DeviceIdType.MESH,
        )

    def each(action):
        def step(ahead, carry):
            action(copy(ahead, lax.rem(me + ahead, count)))
            return carry

        lax.fori_loop(1, count, step, 0)

    def start(ahead):
        copy(ahead, lax.rem(me + ahead, count)).start()

    def start_all():
        each(lambda one: one.start())
        target[me] = source[me]

    return start, start_all, lambda: each(lambda one: one.wait_recv()), lambda: each(lambda one: one.wait_send())


def greet():
    barrier = pltpu.get_barrier_semaphore()
    for axis, count in (("wide", WIDE), ("narrow", NARROW)):
        me = lax.axis_index(axis)

        def step(ahead, carry):
            pl.semaphore_signal(
                barrier,
                inc=1,
                device_id={axis: lax.rem(me + ahead, count)},
                device_id_type=pl.DeviceIdType.MESH,
            )
            return carry

        lax.fori_loop(1, count, step, 0)
    return lambda: pl.semaphore_wait(barrier, WIDE + NARROW - 2)


def entry_phases(received_ref, table, phases):
    cell_z = received_ref[...].reshape(ENTRIES, 2 * C)[:, C + 1 : C + 2].astype(F32)
    position = lax.broadcasted_iota(jnp.int32, (ENTRIES, G), 1).astype(F32)
    at_z = jnp.where(position == cell_z, 1.0, 0.0).astype(BF)
    phases[...] = dot(at_z, table[...]).astype(BF)


def forward_z(received_ref, table, out, own_out, latent, start):
    received = received_ref[...].reshape(ENTRIES, 2 * C)
    cell_row, cell_z, row_xy, row_z = entry_cells(received)
    same = (cell_row * G + cell_z) == (row_xy * G + row_z)
    totals = dot(jnp.where(same, 1.0, 0.0).astype(BF), received)
    scale = 1.0 / jnp.maximum(jnp.sqrt(totals[:, C + 2 : C + 3]), 1.0)
    latent[...] = totals * scale
    own = received.astype(F32) * scale
    lane = lax.broadcasted_iota(jnp.int32, own.shape, 1)
    own = jnp.where(lane < C, own, pltpu.roll(own, C, 1))
    position = lax.broadcasted_iota(jnp.int32, (ENTRIES, G), 1).astype(F32)
    at_z = jnp.where(position == cell_z, 1.0, 0.0).astype(BF)
    pencil = lax.broadcasted_iota(jnp.int32, (XL * YL, ENTRIES), 0).astype(F32)
    at_row = jnp.where(pencil == row_xy, 1.0, 0.0).astype(BF)
    width = KZ * 2 * C
    spread = jnp.concatenate([own] * KZ, axis=1)
    me = lax.axis_index("narrow")
    for ahead in FAR_FIRST + (NARROW,):
        group = lax.rem(me + ahead, NARROW)
        phases = dot(at_z, table[:, pl.ds(pl.multiple_of(group * width, width), width)])
        modes = dot(at_row, (spread * phases).astype(BF)).astype(BF)
        place = out if ahead < NARROW else own_out
        for x in range(XL):
            place[group, :, x * width : (x + 1) * width] = modes[x * YL : (x + 1) * YL, :]
        if ahead < NARROW:
            start(ahead)


def forward_y(received, table, out, columns):
    both = dot(table[...], received[...].reshape(G, XL * KZ * 2 * C))
    for j in range(XL * KZ):
        lanes = slice(j * 2 * C, (j + 1) * 2 * C)
        columns[pl.ds(j, M, stride=XL * KZ), :] = both[0:M, lanes] - turned(both[M:, lanes])
    out[...] = columns[...].astype(BF).reshape(out.shape)


def mix_x(received, forward, inverse, weight, out, left, product):
    count = M * 2 * KZ
    both = dot(forward[...], received[...].reshape(G * KZ, 2 * C))
    modes = both[0:count] - turned(both[count:])
    row = lax.broadcasted_iota(jnp.int32, (count, 2 * C), 0)
    lane = lax.broadcasted_iota(jnp.int32, (count, 2 * C), 1)
    real_row = (row // KZ) % 2 == 0
    wide = jnp.where(real_row == (lane < C), modes, pltpu.roll(modes, C, 1))
    for half in range(KZ // 2):
        keep = row % KZ == 2 * half + lane // C
        left[:, half * 2 * C : (half + 1) * 2 * C] = jnp.where(keep, wide, 0.0)
    for kx in range(M):
        rows = slice(kx * 2 * KZ, (kx + 1) * 2 * KZ)
        product[rows, :] = dot(left[rows, :].astype(BF), weight[kx])
    back = dot(inverse[...], product[...].astype(BF))
    cells = G * KZ
    out[...] = (back[0:cells] + turned(back[cells:])).astype(BF).reshape(out.shape)


def inverse_y(received, table, out, columns):
    columns[...] = received[...].reshape(M * XL * KZ, 2 * C).astype(F32)
    for j in range(XL * KZ):
        column = columns[pl.ds(j, M, stride=XL * KZ), :].astype(BF)
        both = dot(table[...], column)
        value = both[0:G] + turned(both[G:])
        out[:, :, j * 2 * C : (j + 1) * 2 * C] = value.astype(BF).reshape(NARROW, YL, 2 * C)


def inverse_z(received_ref, linear, spectra, phases, out):
    cell_row = received_ref[...].reshape(ENTRIES, 2 * C)[:, C : C + 1].astype(F32)
    pencil = lax.broadcasted_iota(jnp.int32, (ENTRIES, XL * YL), 1).astype(F32)
    at_row = jnp.where(pencil == cell_row, 1.0, 0.0).astype(BF)
    width = KZ * 2 * C
    total = jnp.zeros((ENTRIES, 2 * C), F32)
    for group in range(NARROW):
        pencils = jnp.concatenate(
            [spectra[group, :, x * width : (x + 1) * width] for x in range(XL)], axis=0
        )
        terms = phases[:, group * width : (group + 1) * width].astype(F32) * dot(at_row, pencils)
        for j in range(KZ):
            total += terms[:, j * 2 * C : (j + 1) * 2 * C]
    spectral = total[:, 0:C] + total[:, C:]
    field = half_gelu(0.5 * (spectral + linear[...]))
    field = jnp.concatenate([field, jnp.zeros_like(field)], axis=1)
    out[...] = field.astype(BF).reshape(out.shape)


FAR_FIRST = (4, 3, 5, 2, 6, 1, 7)
WIDE_BUFFER = (WIDE, SLOTS, 2 * C)
NARROW_BUFFER = (NARROW, YL, XL * KZ * 2 * C)
WIDTH = XL * KZ * 2 * C

I32 = jnp.int32
NETWORK = dict(in_w=((6, H), BF), in_b=((1, H), F32), mid_w=((H, H), BF), mid_b=((1, H), F32), out_w=((C, H), BF))
LAYERS = dict(turned_w=((H, H), F32), first=((H, H), BF), second=((H, H), BF), second_b=((H, ROWS), F32))
BLOCK_INPUTS = dict(
    owner=((1, BLKS), I32),
    cell=((1, BLKS), I32),
    fill=((1, BLKS), I32),
    feats=((C, PTS), BF),
    point_proj=((C, C), BF),
)
EDGE_INPUTS = dict(offsets=((3, BLKS * ROWS), F32), points=((BLKS, ROWS), I32))
GRID_INPUTS = dict(
    cell_proj=((C, C), BF),
    skip=((C, C), F32),
    skip_b=((1, C), F32),
    table_z=((G, M * 2 * C), BF),
    forward_y=((2 * M, G), BF),
    forward_x=((4 * M * KZ, G * KZ), BF),
    inverse_x=((2 * G * KZ, 2 * M * KZ), BF),
    inverse_y=((2 * G, M), BF),
    spectral=((M, KZ, C, 2 * C), F32),
)
SCRATCH = dict(
    sent=(WIDE_BUFFER, BF),
    entries=(WIDE_BUFFER, BF),
    pencils=(NARROW_BUFFER, BF),
    columns=(NARROW_BUFFER, BF),
    y_modes=(WIDE_BUFFER, BF),
    slabs=(WIDE_BUFFER, BF),
    mixed=(WIDE_BUFFER, BF),
    rows=(WIDE_BUFFER, BF),
    grid=(NARROW_BUFFER, BF),
    spectra=(NARROW_BUFFER, BF),
    reply=(WIDE_BUFFER, BF),
    returned=(WIDE_BUFFER, BF),
    work=((M * XL * KZ, 2 * C), F32),
    latent=((ENTRIES, 2 * C), F32),
    linear=((ENTRIES, C), F32),
    phases=((ENTRIES, M * 2 * C), BF),
    left=((M * 2 * KZ, KZ * C), F32),
    product=((M * 2 * KZ, 2 * C), F32),
    mixer=((M, KZ * C, 2 * C), BF),
    grouped=((HIGH * C, LOW), BF),
    sums=((BLKS, 2 * C), F32),
    blocks=((BLKS, 2 * C), F32),
    placer=((ENTRIES, BLKS), BF),
    picker=((BLKS, ENTRIES), BF),
    features=((16, LANES), F32),
    weights=((STEPS, C, LANES), F32),
    gathered=((BLKS, C), F32),
    totals=((HIGH * C + 16, LOW), F32),
)
INPUT_GROUPS = (BLOCK_INPUTS, NETWORK, EDGE_INPUTS, NETWORK, GRID_INPUTS)
INPUTS = [item for group in INPUT_GROUPS for item in group.values()]
SCRATCH_GROUPS = INPUT_GROUPS + (LAYERS, LAYERS, SCRATCH)


def whole_body(*refs):
    count = len(INPUTS)
    out = refs[count]
    in_sem, wide_send, wide_recv, narrow_send, narrow_recv = refs[-5:]
    rest = iter(refs[count + 1 : -5])
    held = [types.SimpleNamespace(**{name: next(rest) for name in group}) for group in SCRATCH_GROUPS]
    block, enc, edge, dec, grid, enc_layers, dec_layers, v = held
    places = refs[count + 1 : 2 * count + 1]
    copies = [pltpu.make_async_copy(refs[i], places[i], in_sem.at[i]) for i in range(count)]
    ends = np.cumsum([len(group) for group in INPUT_GROUPS])
    for one in copies[: ends[2]]:
        one.start()
    all_in = greet()

    def need(low, high):
        for one in copies[low:high]:
            one.wait()

    def layers(raw, made):
        prepare_network(
            raw.in_w, raw.in_b, raw.mid_w, raw.mid_b, made.turned_w, made.first, made.second, made.second_b
        )
        return made.first, made.second, made.second_b, raw.out_w

    need(0, ends[1])
    prepare_blocks(block.owner, block.cell, block.fill, v.blocks)
    v.sums[...] = v.blocks[...]
    encoder = layers(enc, enc_layers)
    project_points(block.point_proj, block.feats, v.grouped)
    make_placer(block.owner, v.blocks, v.placer)
    need(ends[1], ends[2])
    for one in copies[ends[2] :]:
        one.start()

    def encode(step, carry):
        encode_chunk(step, edge.offsets, edge.points, v.blocks, v.features, v.grouped, encoder, v.sums)
        return carry

    lax.fori_loop(0, STEPS, encode, 0)
    v.sent[...] = dot(v.placer[...], v.sums[...].astype(BF)).astype(BF).reshape(v.sent.shape)
    all_in()

    def wide(number, source, target):
        return exchange("wide", WIDE, source, target, wide_send.at[number], wide_recv.at[number])

    def narrow(number, source, target):
        return exchange("narrow", NARROW, source, target, narrow_send.at[number], narrow_recv.at[number])

    _, start, receive, finish_entries = wide(0, v.sent, v.entries)
    start()
    need(ends[2], ends[4])
    decoder = layers(dec, dec_layers)

    def weigh(low, high):
        def step_body(step, carry):
            inputs, _ = chunk_inputs(step, edge.offsets, v.blocks, v.features)
            v.weights[step] = network(*decoder, inputs)
            return carry

        lax.fori_loop(low, high, step_body, 0)

    weigh(0, 1)
    receive()

    start_one, _, receive, finish_pencils = narrow(0, v.pencils, v.columns)
    forward_z(v.entries, grid.table_z, v.pencils, v.columns, v.latent, start_one)
    finish_entries()
    linear = jnp.dot(
        v.latent[:, 0:C], grid.skip[...], precision=lax.Precision.HIGHEST, preferred_element_type=F32
    )
    v.linear[...] = linear + grid.skip_b[...]
    weigh(1, 2)
    receive()

    forward_y(v.columns, grid.forward_y, v.y_modes, v.work)
    _, start, receive, finish_modes = wide(1, v.y_modes, v.slabs)
    start()
    finish_pencils()
    v.mixer[...] = grid.spectral[...].reshape(M, KZ * C, 2 * C).astype(BF)
    weigh(2, 3)
    receive()

    mix_x(v.slabs, grid.forward_x, grid.inverse_x, v.mixer, v.mixed, v.left, v.product)
    _, start, receive, finish_mixed = wide(2, v.mixed, v.rows)
    start()
    finish_modes()
    entry_phases(v.entries, grid.table_z, v.phases)
    make_picker(block.owner, v.blocks, v.picker)
    receive()

    inverse_y(v.rows, grid.inverse_y, v.grid, v.work)
    start_one, _, receive, finish_grid = narrow(1, v.grid, v.spectra)
    for ahead in FAR_FIRST:
        start_one(ahead)
    narrow_here = lax.axis_index("narrow")
    v.spectra[narrow_here] = v.grid[narrow_here]
    finish_mixed()
    weigh(3, STEPS)
    receive()

    inverse_z(v.entries, v.linear, v.spectra, v.phases, v.reply)
    _, start, receive, finish_reply = wide(3, v.reply, v.returned)
    start()
    finish_grid()
    v.totals[...] = jnp.zeros_like(v.totals)
    receive()
    unpack_values(v.picker, v.returned, grid.cell_proj, v.gathered)

    def decode(step, carry):
        decode_chunk(step, edge.points, v.blocks, v.weights, v.gathered, v.totals)
        return carry

    lax.fori_loop(0, STEPS, decode, 0)
    finish_points(v.totals, out)
    finish_reply()


def whole_call():
    scratch = [item for group in SCRATCH_GROUPS for item in group.values()]
    return pl.pallas_call(
        whole_body,
        out_shape=jax.ShapeDtypeStruct((C, PTS), BF),
        in_specs=[pl.BlockSpec(memory_space=pl.ANY)] * len(INPUTS),
        out_specs=pl.BlockSpec(memory_space=pltpu.VMEM),
        scratch_shapes=[pltpu.VMEM(shape, kind) for shape, kind in scratch]
        + [
            pltpu.SemaphoreType.DMA((len(INPUTS),)),
            pltpu.SemaphoreType.DMA((4, WIDE)),
            pltpu.SemaphoreType.DMA((4, WIDE)),
            pltpu.SemaphoreType.DMA((2, NARROW)),
            pltpu.SemaphoreType.DMA((2, NARROW)),
        ],
        compiler_params=pltpu.CompilerParams(
            collective_id=0, has_side_effects=True, vmem_limit_bytes=60 * 1024 * 1024
        ),
        name="whole",
    )


def shards(
    point_feats,
    edge_offset,
    edge_point,
    block_fill,
    block_owner,
    block_cell,
    enc_in_w,
    enc_in_b,
    enc_mid_w,
    enc_mid_b,
    enc_out_w,
    point_proj,
    dec_in_w,
    dec_in_b,
    dec_mid_w,
    dec_mid_b,
    dec_out_w,
    cell_proj,
    skip_weight,
    skip_bias,
    spectral_weight,
):
    tables = (z_table(), y_forward_table(), x_forward_table(), x_inverse_table(), y_inverse_table())
    return whole_call()(
        block_owner.reshape(1, BLKS),
        block_cell[None, :],
        block_fill[None, :],
        point_feats,
        point_proj,
        enc_in_w.T,
        enc_in_b[None, :],
        enc_mid_w,
        enc_mid_b[None, :],
        enc_out_w,
        edge_offset,
        edge_point,
        dec_in_w.T,
        dec_in_b[None, :],
        dec_mid_w,
        dec_mid_b[None, :],
        dec_out_w,
        cell_proj,
        skip_weight,
        skip_bias[None, :],
        *[jnp.asarray(table) for table in tables],
        spectral_weight[0],
    )


def solution(mesh):
    return jax.shard_map(
        shards,
        mesh=mesh,
        in_specs=(
            P(None, ("wide", "narrow")),
            P(None, ("wide", "narrow")),
            P(("wide", "narrow"), None),
            P(("wide", "narrow")),
            P(("wide", "narrow"), None),
            P(("wide", "narrow")),
            P(),
            P(),
            P(),
            P(),
            P(),
            P(),
            P(),
            P(),
            P(),
            P(),
            P(),
            P(),
            P(),
            P(),
            P("wide", None, "narrow", None, None),
        ),
        out_specs=P(None, ("wide", "narrow")),
        check_vma=False,
    )
```

```python
import math
import types

import jax
import jax.numpy as jnp
import numpy as np
from jax import lax
from jax.experimental import pallas as pl
from jax.experimental.pallas import tpu as pltpu
from jax.sharding import PartitionSpec as P

G = 128
M = 32
C = 64
H = 128
ROWS = 128
WIDE = 32
NARROW = 8
SLOTS = 16
ENTRIES = WIDE * SLOTS
XL = G // WIDE
YL = G // NARROW
KZ = M // NARROW
PTS = 2048
BLKS = 256
LOW = 256
HIGH = PTS // LOW
STEP_BLKS = 64
LANES = STEP_BLKS * ROWS
STEPS = BLKS // STEP_BLKS
BF = jnp.bfloat16
F32 = jnp.float32

NT = (((1,), (1,)), ((), ()))
TN = (((0,), (0,)), ((), ()))


def dot(left, right, dims=(((1,), (0,)), ((), ()))):
    return lax.dot_general(left, right, dims, preferred_element_type=F32)


def angles(positions, waves):
    return 2.0 * np.pi * (np.outer(positions, waves) % G) / G


WAVES = np.arange(M) - M // 2


def z_table():
    turn = angles(np.arange(G), WAVES)
    both = np.stack([np.cos(turn), -np.sin(turn)], axis=2)
    return np.repeat(both.reshape(G, 2 * M), C, axis=1).astype(BF)


def y_forward_table():
    turn = angles(WAVES, np.arange(G))
    return np.concatenate([np.cos(turn), np.sin(turn)], axis=0).astype(BF)


def y_inverse_table():
    turn = angles(np.arange(G), WAVES)
    return np.concatenate([np.cos(turn), np.sin(turn)], axis=0).astype(BF)


def x_forward_table():
    turn = angles(WAVES, np.arange(G))
    same = np.eye(KZ)
    halves = []
    for wave in (np.cos(turn), np.sin(turn)):
        full = np.einsum("ix,kl->ikxl", wave, same)
        full = np.repeat(full[:, None], 2, axis=1)
        halves.append(full.reshape(M * 2 * KZ, G * KZ))
    return np.concatenate(halves, axis=0).astype(BF)


def x_inverse_table():
    turn = angles(np.arange(G), WAVES)
    same = np.eye(KZ)
    cos, sin = np.cos(turn) / M**3, np.sin(turn) / M**3
    halves = []
    for first, second in ((cos, -sin), (sin, cos)):
        full = np.einsum("xis,kl->xkisl", np.stack([first, second], axis=2), same)
        halves.append(full.reshape(G * KZ, M * 2 * KZ))
    return np.concatenate(halves, axis=0).astype(BF)


def half_gelu(half):
    slope = math.sqrt(2.0 / math.pi)
    inner = half * (half * half * (8.0 * slope * 0.044715) + 2.0 * slope)
    return half + half * jnp.tanh(inner)


def turned(value):
    lane = lax.broadcasted_iota(jnp.int32, value.shape, 1)
    rolled = pltpu.roll(value, C, 1)
    return jnp.where(lane < C, -rolled, rolled)


def prepare_network(in_w, in_b, mid_w, mid_b, turned_w, first, second, second_b):
    bias = 0.5 * in_b[...]
    high = bias.astype(BF).astype(F32)
    number = lax.broadcasted_iota(jnp.int32, (H, H), 0)
    turned_w[...] = jnp.where(number == 6, high, jnp.where(number == 7, bias - high, 0.0))
    turned_w[0:6, :] = 0.5 * in_w[...].astype(F32)
    first[...] = turned_w[...].T.astype(BF)
    second[...] = (0.5 * mid_w[...].astype(F32)).astype(BF)
    second_b[...] = jnp.broadcast_to(0.5 * mid_b[...], (H, H)).T


def network(first, second, second_b, third_w, features):
    hidden = half_gelu(dot(first[:, 0:16], features)).astype(BF)
    bias = jnp.concatenate([second_b[...]] * (features.shape[1] // ROWS), axis=1)
    hidden = half_gelu(dot(second[...], hidden) + bias).astype(BF)
    return dot(third_w[...], hidden)


FILL, OWNER, META = 8, 9, C


def prepare_blocks(owner, cell, fill, blocks):
    cell_row, cell_z = cell[...] >> 7, cell[...] & (G - 1)
    coord_x = owner[...] * XL + (cell_row >> 4)
    coord_y = lax.axis_index("narrow") * YL + (cell_row & (YL - 1))
    number = lax.broadcasted_iota(jnp.int32, (2 * C, BLKS), 0)
    facts = jnp.where((number == 6) | (number == 7), 1.0, 0.0)
    rows = [(3 + i, (2.0 * at.astype(F32) + 1.0) / G - 1.0) for i, at in enumerate((coord_x, coord_y, cell_z))]
    rows += [(FILL, fill[...]), (OWNER, owner[...]), (META, cell_row), (META + 1, cell_z), (META + 2, fill[...])]
    for place, value in rows:
        facts = jnp.where(number == place, value.astype(F32), facts)
    blocks[...] = facts.T


def block_lanes():
    lane = lax.broadcasted_iota(jnp.int32, (STEP_BLKS, LANES), 1)
    return lane - lax.broadcasted_iota(jnp.int32, (STEP_BLKS, LANES), 0) * ROWS


def edge_features(offsets, facts, distance, features_ref):
    inside = jnp.where((distance >= 0) & (distance < ROWS), 1.0, 0.0).astype(BF)
    features_ref[...] = dot(facts[:, 0:16].astype(BF), inside, TN)
    features_ref[0:3, :] = offsets
    return features_ref[...].astype(BF)


def live_lanes(facts, distance):
    fill = facts[:, FILL : FILL + 1].astype(jnp.int32)
    return jnp.where((distance >= 0) & (distance < fill), 1.0, 0.0)


def chunk(step):
    return pl.ds(pl.multiple_of(step * STEP_BLKS, STEP_BLKS), STEP_BLKS)


def point_row(points):
    return jnp.concatenate([points[i : i + 1, :] for i in range(STEP_BLKS)], axis=1)


def low_onehot(row):
    low = jnp.broadcast_to((row & (LOW - 1)).astype(F32), (16, LANES)).astype(BF)
    low = jnp.concatenate([low] * (LOW // 16), axis=0)
    number = lax.broadcasted_iota(jnp.int32, (LOW, LANES), 0).astype(F32).astype(BF)
    return jnp.where(low == number, jnp.ones((), BF), jnp.zeros((), BF))


def project_points(proj, feats, grouped):
    projected = dot(proj[...], feats[...]).astype(BF)
    for high in range(HIGH):
        grouped[high * C : (high + 1) * C, :] = projected[:, high * LOW : (high + 1) * LOW]


def chunk_inputs(step, offsets, blocks, features):
    facts = blocks[chunk(step), :]
    distance = block_lanes()
    lanes = pl.ds(pl.multiple_of(step * LANES, LANES), LANES)
    return edge_features(offsets[:, lanes], facts, distance, features), live_lanes(facts, distance)


PIECES = 16
PIECE = LANES // PIECES


def pick_high(spread, high_row):
    high_row = jnp.broadcast_to(high_row, (C, high_row.shape[1]))
    picked = spread[0:C]
    for high in range(1, HIGH):
        picked = jnp.where(high_row == high, spread[high * C : (high + 1) * C], picked)
    return picked


def encode_chunk(step, offsets, points, blocks, features, grouped, layers, sums):
    first, second, second_b, third = layers
    row = point_row(points[chunk(step), :])
    high_row = row >> 8
    onehot = low_onehot(row)
    inputs, live = chunk_inputs(step, offsets, blocks, features)
    bias = jnp.concatenate([second_b[...]] * (PIECE // ROWS), axis=1)
    raw, hidden, deep, weight, spread, message = {}, {}, {}, {}, {}, {}
    for tick in range(PIECES + 5):
        at = [tick - age if 0 <= tick - age < PIECES else None for age in range(6)]
        lanes = [None if piece is None else slice(piece * PIECE, (piece + 1) * PIECE) for piece in at]
        if at[1] is not None:
            hidden[at[1]] = half_gelu(raw.pop(at[1])).astype(BF)
        if at[3] is not None:
            deep[at[3]] = half_gelu(deep[at[3]] + bias).astype(BF)
        if at[5] is not None:
            picked = pick_high(spread.pop(at[5]), high_row[:, lanes[5]])
            message[at[5]] = (weight.pop(at[5]) * picked).astype(BF)
        if at[0] is not None:
            raw[at[0]] = dot(first[:, 0:16], inputs[:, lanes[0]])
            spread[at[0]] = dot(grouped[...], onehot[:, lanes[0]])
        if at[2] is not None:
            deep[at[2]] = dot(second[...], hidden.pop(at[2]))
        if at[4] is not None:
            weight[at[4]] = dot(third[...], deep.pop(at[4]))
    messages = jnp.concatenate([message[piece] for piece in range(PIECES)], axis=1)
    sums[chunk(step), 0:C] = dot(live.astype(BF), messages, NT)


def make_placer(owner, blocks, placer):
    before = lax.broadcasted_iota(jnp.int32, (BLKS, BLKS), 0) < lax.broadcasted_iota(
        jnp.int32, (BLKS, BLKS), 1
    )
    same = blocks[:, OWNER : OWNER + 1].astype(jnp.int32) == owner[...]
    rank = jnp.sum(jnp.where(same & before, 1, 0), axis=0, keepdims=True)
    target = owner[...] * SLOTS + rank
    slot = lax.broadcasted_iota(jnp.int32, (ENTRIES, BLKS), 0)
    placer[...] = jnp.where(slot == target, 1.0, 0.0).astype(BF)


def make_picker(owner, blocks, picker):
    before = lax.broadcasted_iota(jnp.int32, (BLKS, BLKS), 1) < lax.broadcasted_iota(
        jnp.int32, (BLKS, BLKS), 0
    )
    own = blocks[:, OWNER : OWNER + 1].astype(jnp.int32)
    rank = jnp.sum(jnp.where((own == owner[...]) & before, 1, 0), axis=1, keepdims=True)
    target = own * SLOTS + rank
    slot = lax.broadcasted_iota(jnp.int32, (BLKS, ENTRIES), 1)
    picker[...] = jnp.where(slot == target, 1.0, 0.0).astype(BF)


def unpack_values(picker, returned, proj, gathered):
    values = dot(picker[...], returned[...].reshape(ENTRIES, 2 * C)).astype(BF)
    gathered[...] = dot(values[:, 0:C], proj[...], NT)


def decode_chunk(step, points, blocks, weights, gathered, totals):
    alive = jnp.sum(live_lanes(blocks[chunk(step), :], block_lanes()), axis=0, keepdims=True)
    cells = gathered[chunk(step), :]
    cells = jnp.concatenate([cells, cells], axis=1)
    cells = jnp.concatenate([cells] * (ROWS // STEP_BLKS), axis=0).T
    spread = jnp.concatenate(
        [jnp.broadcast_to(cells[0:C, i : i + 1], (C, ROWS)) for i in range(STEP_BLKS)], axis=1
    )
    message = (weights[step] * spread).astype(BF)
    row = jnp.where(alive > 0.5, point_row(points[chunk(step), :]), -1)
    high = jnp.broadcast_to((row >> 8).astype(F32), (16, LANES)).astype(BF)
    high_rows = jnp.concatenate([high] * (C // 16), axis=0)
    parts = [jnp.where(high_rows == jnp.full((), i, BF), message, jnp.zeros((), BF)) for i in range(HIGH)]
    number = lax.broadcasted_iota(jnp.int32, (16, LANES), 0)
    parts.append(jnp.where(number == row >> 8, 1.0, 0.0).astype(BF))
    totals[...] += dot(jnp.concatenate(parts, axis=0), low_onehot(row), NT)


def finish_points(totals, out):
    for high in range(HIGH):
        degree = totals[HIGH * C + high : HIGH * C + high + 1, :]
        scale = 1.0 / jnp.maximum(jnp.sqrt(degree), 1.0)
        value = totals[high * C : (high + 1) * C, :] * scale
        out[:, high * LOW : (high + 1) * LOW] = value.astype(BF)


def entry_cells(received):
    cell_row = received[:, C : C + 1].astype(F32)
    cell_z = received[:, C + 1 : C + 2].astype(F32)
    lane = lax.broadcasted_iota(jnp.int32, (16, 2 * C), 1)
    sub = lax.broadcasted_iota(jnp.int32, (16, 2 * C), 0)
    picker = jnp.where(lane == sub + C, 1.0, 0.0).astype(BF)
    rows = dot(picker, received, NT)
    return cell_row, cell_z, rows[0:1, :], rows[1:2, :]


def exchange(axis, count, source, target, send_sem, recv_sem):
    me = lax.axis_index(axis)

    def copy(ahead, peer):
        return pltpu.make_async_remote_copy(
            src_ref=source.at[peer],
            dst_ref=target.at[me],
            send_sem=send_sem.at[ahead],
            recv_sem=recv_sem.at[ahead],
            device_id={axis: peer},
            device_id_type=pl.DeviceIdType.MESH,
        )

    def each(action):
        def step(ahead, carry):
            action(copy(ahead, lax.rem(me + ahead, count)))
            return carry

        lax.fori_loop(1, count, step, 0)

    def start(ahead):
        copy(ahead, lax.rem(me + ahead, count)).start()

    def arrive(ahead):
        copy(ahead, lax.rem(me + ahead, count)).wait_recv()

    def start_all():
        each(lambda one: one.start())
        target[me] = source[me]

    finish = lambda: each(lambda one: one.wait_send())
    return start, start_all, arrive, lambda: each(lambda one: one.wait_recv()), finish


def greet():
    barrier = pltpu.get_barrier_semaphore()
    for axis, count in (("wide", WIDE), ("narrow", NARROW)):
        me = lax.axis_index(axis)

        def step(ahead, carry):
            pl.semaphore_signal(
                barrier,
                inc=1,
                device_id={axis: lax.rem(me + ahead, count)},
                device_id_type=pl.DeviceIdType.MESH,
            )
            return carry

        lax.fori_loop(1, count, step, 0)
    return lambda: pl.semaphore_wait(barrier, WIDE + NARROW - 2)


def entry_phases(received_ref, table, phases):
    cell_z = received_ref[...].reshape(ENTRIES, 2 * C)[:, C + 1 : C + 2].astype(F32)
    position = lax.broadcasted_iota(jnp.int32, (ENTRIES, G), 1).astype(F32)
    at_z = jnp.where(position == cell_z, 1.0, 0.0).astype(BF)
    phases[...] = dot(at_z, table[...]).astype(BF)


def forward_z(received_ref, table, out, own_out, latent, start):
    received = received_ref[...].reshape(ENTRIES, 2 * C)
    cell_row, cell_z, row_xy, row_z = entry_cells(received)
    same = (cell_row * G + cell_z) == (row_xy * G + row_z)
    totals = dot(jnp.where(same, 1.0, 0.0).astype(BF), received)
    scale = 1.0 / jnp.maximum(jnp.sqrt(totals[:, C + 2 : C + 3]), 1.0)
    latent[...] = totals * scale
    own = received.astype(F32) * scale
    lane = lax.broadcasted_iota(jnp.int32, own.shape, 1)
    own = jnp.where(lane < C, own, pltpu.roll(own, C, 1))
    position = lax.broadcasted_iota(jnp.int32, (ENTRIES, G), 1).astype(F32)
    at_z = jnp.where(position == cell_z, 1.0, 0.0).astype(BF)
    pencil = lax.broadcasted_iota(jnp.int32, (XL * YL, ENTRIES), 0).astype(F32)
    at_row = jnp.where(pencil == row_xy, 1.0, 0.0).astype(BF)
    width = KZ * 2 * C
    spread = jnp.concatenate([own] * KZ, axis=1)
    me = lax.axis_index("narrow")
    for ahead in FAR_FIRST + (NARROW,):
        group = lax.rem(me + ahead, NARROW)
        phases = dot(at_z, table[:, pl.ds(pl.multiple_of(group * width, width), width)])
        modes = dot(at_row, (spread * phases).astype(BF)).astype(BF)
        place = out if ahead < NARROW else own_out
        for x in range(XL):
            place[group, :, x * width : (x + 1) * width] = modes[x * YL : (x + 1) * YL, :]
        if ahead < NARROW:
            start(ahead)


def forward_y(received, table, out, columns):
    both = dot(table[...], received[...].reshape(G, XL * KZ * 2 * C))
    for j in range(XL * KZ):
        lanes = slice(j * 2 * C, (j + 1) * 2 * C)
        columns[pl.ds(j, M, stride=XL * KZ), :] = both[0:M, lanes] - turned(both[M:, lanes])
    out[...] = columns[...].astype(BF).reshape(out.shape)


def mix_x(received, forward, inverse, weight, out, left, product):
    count = M * 2 * KZ
    both = dot(forward[...], received[...].reshape(G * KZ, 2 * C))
    modes = both[0:count] - turned(both[count:])
    row = lax.broadcasted_iota(jnp.int32, (count, 2 * C), 0)
    lane = lax.broadcasted_iota(jnp.int32, (count, 2 * C), 1)
    real_row = (row // KZ) % 2 == 0
    wide = jnp.where(real_row == (lane < C), modes, pltpu.roll(modes, C, 1))
    for half in range(KZ // 2):
        keep = row % KZ == 2 * half + lane // C
        left[:, half * 2 * C : (half + 1) * 2 * C] = jnp.where(keep, wide, 0.0)
    step = 4 * KZ
    for pair in range(M // 2):
        both = dot(left[pair * step : (pair + 1) * step, :].astype(BF), weight[pair])
        for side in range(2):
            rows = slice(side * 2 * KZ, (side + 1) * 2 * KZ)
            place = pl.ds(pair * step + side * 2 * KZ, 2 * KZ)
            product[place, :] = both[rows, side * 2 * C : (side + 1) * 2 * C]
    back = dot(inverse[...], product[...].astype(BF))
    cells = G * KZ
    out[...] = (back[0:cells] + turned(back[cells:])).astype(BF).reshape(out.shape)


def inverse_y(received, table, out, columns):
    columns[...] = received[...].reshape(M * XL * KZ, 2 * C).astype(F32)
    for j in range(XL * KZ):
        column = columns[pl.ds(j, M, stride=XL * KZ), :].astype(BF)
        both = dot(table[...], column)
        value = both[0:G] + turned(both[G:])
        out[:, :, j * 2 * C : (j + 1) * 2 * C] = value.astype(BF).reshape(NARROW, YL, 2 * C)


def inverse_z(received_ref, linear, spectra, phases, out, arrive):
    cell_row = received_ref[...].reshape(ENTRIES, 2 * C)[:, C : C + 1].astype(F32)
    pencil = lax.broadcasted_iota(jnp.int32, (ENTRIES, XL * YL), 1).astype(F32)
    at_row = jnp.where(pencil == cell_row, 1.0, 0.0).astype(BF)
    width = KZ * 2 * C
    total = jnp.zeros((ENTRIES, 2 * C), F32)
    me = lax.axis_index("narrow")
    for ahead in (0,) + FAR_FIRST[::-1]:
        if ahead > 0:
            arrive(ahead)
        group = lax.rem(me - ahead + NARROW, NARROW)
        pencils = jnp.concatenate(
            [spectra[group, :, x * width : (x + 1) * width] for x in range(XL)], axis=0
        )
        turn = phases[:, pl.ds(pl.multiple_of(group * width, width), width)]
        terms = turn.astype(F32) * dot(at_row, pencils)
        for j in range(KZ):
            total += terms[:, j * 2 * C : (j + 1) * 2 * C]
    spectral = total[:, 0:C] + total[:, C:]
    field = half_gelu(0.5 * (spectral + linear[...]))
    field = jnp.concatenate([field, jnp.zeros_like(field)], axis=1)
    out[...] = field.astype(BF).reshape(out.shape)


FAR_FIRST = (4, 3, 5, 2, 6, 1, 7)
WIDE_BUFFER = (WIDE, SLOTS, 2 * C)
NARROW_BUFFER = (NARROW, YL, XL * KZ * 2 * C)
WIDTH = XL * KZ * 2 * C

I32 = jnp.int32
NETWORK = dict(in_w=((6, H), BF), in_b=((1, H), F32), mid_w=((H, H), BF), mid_b=((1, H), F32), out_w=((C, H), BF))
LAYERS = dict(turned_w=((H, H), F32), first=((H, H), BF), second=((H, H), BF), second_b=((H, ROWS), F32))
BLOCK_INPUTS = dict(
    owner=((1, BLKS), I32),
    cell=((1, BLKS), I32),
    fill=((1, BLKS), I32),
    feats=((C, PTS), BF),
    point_proj=((C, C), BF),
)
EDGE_INPUTS = dict(offsets=((3, BLKS * ROWS), F32), points=((BLKS, ROWS), I32))
GRID_INPUTS = dict(
    cell_proj=((C, C), BF),
    skip=((C, C), F32),
    skip_b=((1, C), F32),
    table_z=((G, M * 2 * C), BF),
    forward_y=((2 * M, G), BF),
    forward_x=((4 * M * KZ, G * KZ), BF),
    inverse_x=((2 * G * KZ, 2 * M * KZ), BF),
    inverse_y=((2 * G, M), BF),
    spectral=((M, KZ, C, 2 * C), F32),
)
SCRATCH = dict(
    sent=(WIDE_BUFFER, BF),
    entries=(WIDE_BUFFER, BF),
    pencils=(NARROW_BUFFER, BF),
    columns=(NARROW_BUFFER, BF),
    y_modes=(WIDE_BUFFER, BF),
    slabs=(WIDE_BUFFER, BF),
    mixed=(WIDE_BUFFER, BF),
    rows=(WIDE_BUFFER, BF),
    grid=(NARROW_BUFFER, BF),
    spectra=(NARROW_BUFFER, BF),
    reply=(WIDE_BUFFER, BF),
    returned=(WIDE_BUFFER, BF),
    work=((M * XL * KZ, 2 * C), F32),
    latent=((ENTRIES, 2 * C), F32),
    linear=((ENTRIES, C), F32),
    phases=((ENTRIES, M * 2 * C), BF),
    left=((M * 2 * KZ, KZ * C), F32),
    product=((M * 2 * KZ, 2 * C), F32),
    mixer=((M // 2, KZ * C, 4 * C), BF),
    grouped=((HIGH * C, LOW), BF),
    sums=((BLKS, 2 * C), F32),
    blocks=((BLKS, 2 * C), F32),
    placer=((ENTRIES, BLKS), BF),
    picker=((BLKS, ENTRIES), BF),
    features=((16, LANES), F32),
    weights=((STEPS, C, LANES), F32),
    gathered=((BLKS, C), F32),
    totals=((HIGH * C + 16, LOW), F32),
)
INPUT_GROUPS = (BLOCK_INPUTS, NETWORK, EDGE_INPUTS, NETWORK, GRID_INPUTS)
INPUTS = [item for group in INPUT_GROUPS for item in group.values()]
SCRATCH_GROUPS = INPUT_GROUPS + (LAYERS, LAYERS, SCRATCH)


def whole_body(*refs):
    count = len(INPUTS)
    out = refs[count]
    in_sem, wide_send, wide_recv, narrow_send, narrow_recv = refs[-5:]
    rest = iter(refs[count + 1 : -5])
    held = [types.SimpleNamespace(**{name: next(rest) for name in group}) for group in SCRATCH_GROUPS]
    block, enc, edge, dec, grid, enc_layers, dec_layers, v = held
    places = refs[count + 1 : 2 * count + 1]
    copies = [pltpu.make_async_copy(refs[i], places[i], in_sem.at[i]) for i in range(count)]
    ends = np.cumsum([len(group) for group in INPUT_GROUPS])
    for one in copies[: ends[2]]:
        one.start()
    all_in = greet()

    def need(low, high):
        for one in copies[low:high]:
            one.wait()

    def layers(raw, made):
        prepare_network(
            raw.in_w, raw.in_b, raw.mid_w, raw.mid_b, made.turned_w, made.first, made.second, made.second_b
        )
        return made.first, made.second, made.second_b, raw.out_w

    need(0, ends[1])
    prepare_blocks(block.owner, block.cell, block.fill, v.blocks)
    v.sums[...] = v.blocks[...]
    encoder = layers(enc, enc_layers)
    project_points(block.point_proj, block.feats, v.grouped)
    make_placer(block.owner, v.blocks, v.placer)
    need(ends[1], ends[2])
    for one in copies[ends[2] :]:
        one.start()

    def encode(step, carry):
        encode_chunk(step, edge.offsets, edge.points, v.blocks, v.features, v.grouped, encoder, v.sums)
        return carry

    lax.fori_loop(0, STEPS, encode, 0)
    v.sent[...] = dot(v.placer[...], v.sums[...].astype(BF)).astype(BF).reshape(v.sent.shape)
    all_in()

    def wide(number, source, target):
        return exchange("wide", WIDE, source, target, wide_send.at[number], wide_recv.at[number])

    def narrow(number, source, target):
        return exchange("narrow", NARROW, source, target, narrow_send.at[number], narrow_recv.at[number])

    _, start, _, receive, finish_entries = wide(0, v.sent, v.entries)
    start()
    need(ends[2], ends[4])
    decoder = layers(dec, dec_layers)

    def weigh(low, high):
        def step_body(step, carry):
            inputs, _ = chunk_inputs(step, edge.offsets, v.blocks, v.features)
            v.weights[step] = network(*decoder, inputs)
            return carry

        lax.fori_loop(low, high, step_body, 0)

    weigh(0, 1)
    receive()

    start_one, _, _, receive, finish_pencils = narrow(0, v.pencils, v.columns)
    forward_z(v.entries, grid.table_z, v.pencils, v.columns, v.latent, start_one)
    finish_entries()
    linear = jnp.dot(
        v.latent[:, 0:C], grid.skip[...], precision=lax.Precision.HIGHEST, preferred_element_type=F32
    )
    v.linear[...] = linear + grid.skip_b[...]
    weigh(1, 2)
    receive()

    forward_y(v.columns, grid.forward_y, v.y_modes, v.work)
    _, start, _, receive, finish_modes = wide(1, v.y_modes, v.slabs)
    start()
    finish_pencils()
    mixer = grid.spectral[...].reshape(M // 2, 2, KZ * C, 2 * C).astype(BF)
    v.mixer[:, :, 0 : 2 * C] = mixer[:, 0]
    v.mixer[:, :, 2 * C :] = mixer[:, 1]
    weigh(2, 3)
    receive()

    mix_x(v.slabs, grid.forward_x, grid.inverse_x, v.mixer, v.mixed, v.left, v.product)
    _, start, _, receive, finish_mixed = wide(2, v.mixed, v.rows)
    start()
    finish_modes()
    entry_phases(v.entries, grid.table_z, v.phases)
    make_picker(block.owner, v.blocks, v.picker)
    receive()

    inverse_y(v.rows, grid.inverse_y, v.grid, v.work)
    start_one, _, arrive, _, finish_grid = narrow(1, v.grid, v.spectra)
    for ahead in FAR_FIRST:
        start_one(ahead)
    narrow_here = lax.axis_index("narrow")
    v.spectra[narrow_here] = v.grid[narrow_here]
    finish_mixed()
    weigh(3, STEPS)

    inverse_z(v.entries, v.linear, v.spectra, v.phases, v.reply, arrive)
    _, start, _, receive, finish_reply = wide(3, v.reply, v.returned)
    start()
    finish_grid()
    v.totals[...] = jnp.zeros_like(v.totals)
    receive()
    unpack_values(v.picker, v.returned, grid.cell_proj, v.gathered)

    def decode(step, carry):
        decode_chunk(step, edge.points, v.blocks, v.weights, v.gathered, v.totals)
        return carry

    lax.fori_loop(0, STEPS, decode, 0)
    finish_points(v.totals, out)
    finish_reply()


def whole_call():
    scratch = [item for group in SCRATCH_GROUPS for item in group.values()]
    return pl.pallas_call(
        whole_body,
        out_shape=jax.ShapeDtypeStruct((C, PTS), BF),
        in_specs=[pl.BlockSpec(memory_space=pl.ANY)] * len(INPUTS),
        out_specs=pl.BlockSpec(memory_space=pltpu.VMEM),
        scratch_shapes=[pltpu.VMEM(shape, kind) for shape, kind in scratch]
        + [
            pltpu.SemaphoreType.DMA((len(INPUTS),)),
            pltpu.SemaphoreType.DMA((4, WIDE)),
            pltpu.SemaphoreType.DMA((4, WIDE)),
            pltpu.SemaphoreType.DMA((2, NARROW)),
            pltpu.SemaphoreType.DMA((2, NARROW)),
        ],
        compiler_params=pltpu.CompilerParams(
            collective_id=0, has_side_effects=True, vmem_limit_bytes=60 * 1024 * 1024
        ),
        name="whole",
    )


def shards(
    point_feats,
    edge_offset,
    edge_point,
    block_fill,
    block_owner,
    block_cell,
    enc_in_w,
    enc_in_b,
    enc_mid_w,
    enc_mid_b,
    enc_out_w,
    point_proj,
    dec_in_w,
    dec_in_b,
    dec_mid_w,
    dec_mid_b,
    dec_out_w,
    cell_proj,
    skip_weight,
    skip_bias,
    spectral_weight,
):
    tables = (z_table(), y_forward_table(), x_forward_table(), x_inverse_table(), y_inverse_table())
    return whole_call()(
        block_owner.reshape(1, BLKS),
        block_cell[None, :],
        block_fill[None, :],
        point_feats,
        point_proj,
        enc_in_w.T,
        enc_in_b[None, :],
        enc_mid_w,
        enc_mid_b[None, :],
        enc_out_w,
        edge_offset,
        edge_point,
        dec_in_w.T,
        dec_in_b[None, :],
        dec_mid_w,
        dec_mid_b[None, :],
        dec_out_w,
        cell_proj,
        skip_weight,
        skip_bias[None, :],
        *[jnp.asarray(table) for table in tables],
        spectral_weight[0],
    )


def solution(mesh):
    return jax.shard_map(
        shards,
        mesh=mesh,
        in_specs=(
            P(None, ("wide", "narrow")),
            P(None, ("wide", "narrow")),
            P(("wide", "narrow"), None),
            P(("wide", "narrow")),
            P(("wide", "narrow"), None),
            P(("wide", "narrow")),
            P(),
            P(),
            P(),
            P(),
            P(),
            P(),
            P(),
            P(),
            P(),
            P(),
            P(),
            P(),
            P(),
            P(),
            P("wide", None, "narrow", None, None),
        ),
        out_specs=P(None, ("wide", "narrow")),
        check_vma=False,
    )
```
